512 devices in a mesh: ctx: 64 (over z_hi, x, y), ch: 8 (over z_lo, core).
Axes of the slice: x: 4, y: 4, z: 16 (z_hi: 4, z_lo: 4; z = z_hi * 4 + z_lo), core: 2. Of those that a mesh axis runs over, the one named last changes fastest.
Arguments:
- features: bfloat16 [8192, 8192], P('ctx', 'ch'), as said below
- norm_gain: float32 [8192], P('ch'), may hold values from 0.5 to 1.5
- skip_gain: float32 [8192], P('ch'), may hold values from -1 to 1
- gate_value: bfloat16 [8192, 8192], P('ctx', 'ch'), may hold values from -6 to 6
- cotangent: bfloat16 [8192, 8192], P('ctx', 'ch'), may hold values from -6 to 6
- residue: float32 [512, 16], P('ch'), as said below
- log_rate: float32 [512, 16], P('ch'), as said below
Outputs:
- gated_out: bfloat16 [8192, 8192], P('ctx', 'ch')
- grad_residue: float32 [512, 16], P('ch')
- grad_log_rate: float32 [512, 16], P('ch')
The draws below stay inside these ranges and needn't reach their ends.
Inputs may be any that keep to these rules, and one draw needn't show every extreme that they name: `features`: Real-valued activations. `residue`: Real-valued mode weights. exp(log_rate) lies between 0.25 / 8192 and 0.125.
All inputs are finite; a program needn't handle non-finite values.
Results may differ from the reference program's by a relative error of at most 0.0057.
Values may be sent and summed in bfloat16 or wider, within the bound.
A program may use at most 64 MiB of HBM per device.

```python
import math
import jax
import jax.numpy as jnp
from jax import lax

D = 8192
GROUP = 16
MODES = 16
FILTERS = 512
LENGTH = 8192


def mode_rates(key, slow_share):
    slow_pick = jax.random.uniform(jax.random.fold_in(key, 11), (FILTERS, MODES)) < slow_share
    slow_rate = jnp.exp(jax.random.uniform(jax.random.fold_in(key, 12), (FILTERS, MODES), jnp.float32, math.log(0.25 / LENGTH), math.log(2.0 / LENGTH)))
    fast_rate = jnp.exp(jax.random.uniform(jax.random.fold_in(key, 13), (FILTERS, MODES), jnp.float32, math.log(1.0 / 64.0), math.log(0.125)))
    return jnp.where(slow_pick, slow_rate, fast_rate)


def draw_log_rate(key, part):
    slow_share = 0.5
    rate_vals = mode_rates(key, slow_share)
    return jnp.log(rate_vals)


def draw_residue(key, part):
    slow_share = 0.5
    rate_vals = mode_rates(key, slow_share)
    key = jax.random.fold_in(key, 3)
    noise_vals = jax.random.normal(key, (FILTERS, MODES), jnp.float32)
    return noise_vals * jnp.sqrt(2.0 * rate_vals / MODES)


def draw_features(key, part):
    key = jax.random.fold_in(key, 7)
    col_scale = 3.0 ** (jnp.arange(D, dtype=jnp.float32) / D)
    col_scale = col_scale * jnp.exp(jax.random.uniform(jax.random.fold_in(key, 2), (1, D), jnp.float32, math.log(0.7), math.log(1.4)))
    row_scale = jnp.exp(jax.random.uniform(jax.random.fold_in(key, 1), (LENGTH, 1), jnp.float32, 0.0, math.log(10.0)))
    base_vals = jnp.clip(jax.random.normal(jax.random.fold_in(key, 3), (LENGTH, D), jnp.float32), -6.0, 6.0)
    return (base_vals * row_scale * col_scale).astype(jnp.bfloat16)


def shard_levels(key, extent, split, smallest, high):
    def one(position, parts):
        steps = jax.random.uniform(jax.random.fold_in(jax.random.fold_in(key, 6), position), (parts,), jnp.float32, smallest / len(split), high / len(split))
        return jnp.repeat(jnp.exp(steps), extent[position] // parts).reshape((-1,) + (1,) * (len(extent) - position - 1))

    gain = one(*split[0])
    for cut in split[1:]:
        gain = gain * one(*cut)
    return gain


def noise(stream_key, shape, scale, reach, shards=(), kind=jnp.bfloat16):
    result = scale * jax.random.normal(stream_key, shape, jnp.float32)
    if shards:
        result = result * shard_levels(stream_key, shape, shards, -0.22, 0.18)
    return jnp.clip(result, -reach, reach).astype(kind)


def setup_inputs(seed: int = 0) -> dict:
    splits = jax.random.split(jax.random.key(seed), 8)
    features = draw_features(jax.random.fold_in(splits[7], 71), 0)
    norm_gain = jnp.clip(0.5 + 1.0 * jax.random.uniform(splits[1], (D,), jnp.float32) ** shard_levels(splits[1], (D,), ((0, 8),), -0.2, 0.2), 0.5, 1.5)
    skip_gain = jnp.clip(jax.random.uniform(splits[2], (D,), jnp.float32, -1.0, 1.0) * shard_levels(splits[2], (D,), ((0, 8),), -0.4, 0.0), -1.0, 1.0)
    gate_value = noise(splits[3], (LENGTH, D), 1.0, 6.0, ((0, 64), (1, 8)))
    cotangent = noise(splits[4], (LENGTH, D), 1.0, 6.0, ((0, 64), (1, 8)))
    residue = draw_residue(jax.random.fold_in(splits[7], 71), 0)
    log_rate = draw_log_rate(jax.random.fold_in(splits[7], 71), 0)
    return {"features": features, "norm_gain": norm_gain, "skip_gain": skip_gain, "gate_value": gate_value, "cotangent": cotangent, "residue": residue, "log_rate": log_rate}


EPSILON = 1e-06
HIGHEST = lax.Precision.HIGHEST

def reference(features, norm_gain, skip_gain, gate_value, cotangent, residue, log_rate):
    x_float = features.astype(jnp.float32)
    mean_sq = lax.optimization_barrier(jnp.mean(x_float * x_float, axis=1, keepdims=True))
    x_norm = (x_float * lax.rsqrt(mean_sq + EPSILON) * norm_gain.astype(jnp.float32)[None, :]).astype(jnp.bfloat16)
    d_norm = (cotangent.astype(jnp.float32) * gate_value.astype(jnp.float32)).astype(jnp.bfloat16)
    rate_vals = jnp.exp(log_rate)
    block_filters = min(64, FILTERS)
    block_count = FILTERS // block_filters
    block_width = block_filters * GROUP
    x_blocks = x_norm.reshape(LENGTH, block_count, block_width).transpose(1, 0, 2)
    d_blocks = d_norm.reshape(LENGTH, block_count, block_width).transpose(1, 0, 2)
    g_blocks = gate_value.reshape(LENGTH, block_count, block_width).transpose(1, 0, 2)
    skip_blocks = skip_gain.reshape(block_count, block_width)
    rate_blocks = rate_vals.reshape(block_count, block_filters, MODES)
    res_blocks = residue.reshape(block_count, block_filters, MODES)
    lag_axis = jnp.arange(LENGTH, dtype=jnp.float32)
    fft_len = 2 * LENGTH

    def per_block(packed):
        x_block, d_block, g_block, skip_block, rate_block, res_block = packed
        decay_tab = jnp.exp(-rate_block[:, :, None] * lag_axis[None, None, :])
        filter_rows = lax.optimization_barrier(jnp.sum(res_block[:, :, None] * decay_tab, axis=1))
        filter_chan = jnp.repeat(filter_rows, GROUP, axis=0).T
        x_vals = x_block.astype(jnp.float32)
        spectrum = jnp.fft.rfft(x_vals, n=fft_len, axis=0)
        convolved = jnp.fft.irfft(spectrum * jnp.fft.rfft(filter_chan, n=fft_len, axis=0), n=fft_len, axis=0)[:LENGTH]
        conv_out = (convolved + skip_block.astype(jnp.float32)[None, :] * x_vals).astype(jnp.bfloat16)
        gated = (g_block.astype(jnp.float32) * conv_out.astype(jnp.float32)).astype(jnp.bfloat16)
        d_spec = jnp.fft.rfft(d_block.astype(jnp.float32), n=fft_len, axis=0)
        correlated = jnp.fft.irfft(jnp.conj(spectrum) * d_spec, n=fft_len, axis=0)[:LENGTH]
        per_filter = correlated.reshape(LENGTH, block_filters, GROUP).sum(axis=2)
        grad_res = jnp.einsum('kf,fmk->fm', per_filter, decay_tab, precision=HIGHEST) / LENGTH
        grad_lag = jnp.einsum('kf,fmk->fm', per_filter, decay_tab * lag_axis[None, None, :], precision=HIGHEST) / LENGTH
        return (gated, grad_res, -res_block * rate_block * grad_lag)
    gated_all, grad_res_all, grad_rate_all = lax.map(per_block, (x_blocks, d_blocks, g_blocks, skip_blocks, rate_blocks, res_blocks))
    gated_out = gated_all.transpose(1, 0, 2).reshape(LENGTH, D)
    return (gated_out, grad_res_all.reshape(FILTERS, MODES), grad_rate_all.reshape(FILTERS, MODES))
```

```python
import functools

import jax
import jax.numpy as jnp
from jax import lax
from jax.experimental import pallas as pl
from jax.experimental.pallas import tpu as pltpu
from jax.sharding import PartitionSpec as P

EPSILON = 1e-06
HIGHEST = lax.Precision.HIGHEST
F32 = jnp.float32
BF16 = jnp.bfloat16
LANES = 128
MODES = 16
GROUP = 16
PER_TILE = 8
MESH = pl.DeviceIdType.MESH


def iota(shape, axis):
    return lax.broadcasted_iota(jnp.int32, shape, axis)


def nt(a, b, precision=None):
    return lax.dot_general(
        a, b, (((1,), (1,)), ((), ())), precision=precision, preferred_element_type=F32
    )


def nn(a, b, precision=None):
    return lax.dot_general(
        a, b, (((1,), (0,)), ((), ())), precision=precision, preferred_element_type=F32
    )


def split(x):
    high = x.astype(BF16)
    low = (x - high.astype(F32)).astype(BF16)
    return jnp.concatenate([high, low], axis=1)


def own_filter(values):
    lane_filter = iota((MODES, LANES), 1) // GROUP
    kept = values[:MODES]
    for f in range(1, PER_TILE):
        kept = jnp.where(lane_filter == f, values[f * MODES : (f + 1) * MODES], kept)
    return kept


def body(
    plane, planes, groups, length,
    feat_hbm, gain_hbm, skip_hbm, gate_hbm, cot_hbm, res_hbm, lrate_hbm,
    out_ref, gres_ref, grate_ref,
    feat, gain, skip, gate, cot, res, lrate,
    xn, dn, rate_rows, res_rows, w_sum, a_out, decay, y_local, diag,
    sq_out, sq_in, s_out, s_in, c_out, c_in, l_out, l_in,
    z_out, z_in, zg_out, zg_in, r_out, r_in, g_out, g_in,
    pre_one,
    load_sem, send_sem, recv_sem,
):
    rows = feat.shape[0]
    tiles = feat.shape[1] // LANES
    ctx, ch = lax.axis_index("ctx"), lax.axis_index("ch")
    z_me, p_me = ctx // plane, ctx % plane

    loads = [
        pltpu.make_async_copy(src, dst, load_sem.at[n])
        for n, (src, dst) in enumerate(
            (
                (feat_hbm, feat), (lrate_hbm, lrate), (res_hbm, res), (gain_hbm, gain),
                (skip_hbm, skip), (cot_hbm, cot), (gate_hbm, gate),
            )
        )
    ]
    for load in loads:
        load.start()

    def plane_peer(i):
        return (p_me + i) % plane

    def z_peer(i):
        return (z_me + i) % planes

    barrier = pltpu.get_barrier_semaphore()
    for i in range(1, groups):
        pl.semaphore_signal(barrier, inc=1, device_id={"ch": (ch + i) % groups}, device_id_type=MESH)
    for i in range(1, plane):
        pl.semaphore_signal(
            barrier, inc=1, device_id={"ctx": z_me * plane + plane_peer(i)}, device_id_type=MESH
        )
    for i in range(1, planes):
        pl.semaphore_signal(
            barrier, inc=1, device_id={"ctx": z_peer(i) * plane + p_me}, device_id_type=MESH
        )

    def send_plane(src, dst, kind):
        for i in range(1, plane):
            peer = plane_peer(i)
            pltpu.make_async_remote_copy(
                src_ref=src.at[peer], dst_ref=dst.at[p_me],
                send_sem=send_sem.at[kind], recv_sem=recv_sem.at[kind],
                device_id={"ctx": z_me * plane + peer}, device_id_type=MESH,
            ).start()

    def send_z(src, dst, kind):
        for i in range(1, planes):
            pltpu.make_async_remote_copy(
                src_ref=src, dst_ref=dst.at[z_me],
                send_sem=send_sem.at[kind], recv_sem=recv_sem.at[kind],
                device_id={"ctx": z_peer(i) * plane + p_me}, device_id_type=MESH,
            ).start()

    def send_groups(src, dst, kind):
        for i in range(1, groups):
            pltpu.make_async_remote_copy(
                src_ref=src, dst_ref=dst.at[ch],
                send_sem=send_sem.at[kind], recv_sem=recv_sem.at[kind],
                device_id={"ch": (ch + i) % groups}, device_id_type=MESH,
            ).start()

    def wait_in(dst, kind):
        part = dst.at[pl.ds(0, dst.shape[0] - 1)]
        pltpu.make_async_copy(part, part, recv_sem.at[kind]).wait()

    def wait_out(dst, kind):
        part = dst.at[pl.ds(0, dst.shape[0] - 1)]
        pltpu.make_async_copy(part, part, send_sem.at[kind]).wait()

    loads[0].wait()
    squares = jnp.zeros((rows, LANES), F32)
    for j in range(tiles):
        part = feat[:, j * LANES : (j + 1) * LANES].astype(F32)
        squares += part * part
    sq_row = jnp.sum(jnp.transpose(squares), axis=0, keepdims=True)
    sq_out[...] = jnp.broadcast_to(sq_row, sq_out.shape)
    sq_in[ch] = sq_out[...]
    pl.semaphore_wait(barrier, (groups - 1) + (plane - 1) + (planes - 1))
    send_groups(sq_out, sq_in, 0)

    loads[1].wait()
    loads[2].wait()
    lanes_of_mode = (iota((MODES, LANES), 1) % MODES == iota((MODES, LANES), 0)).astype(F32)
    same_filter = iota((PER_TILE, LANES), 1) // MODES == iota((PER_TILE, LANES), 0)
    for j in range(tiles):
        part = slice(j * PER_TILE, (j + 1) * PER_TILE)
        rate_rep = nn(jnp.exp(lrate[part, :]), lanes_of_mode, HIGHEST)
        res_rep = nn(res[part, :], lanes_of_mode, HIGHEST)
        rate_row = jnp.sum(jnp.where(same_filter, rate_rep, 0.0), axis=0, keepdims=True)
        rate_rows[j] = jnp.broadcast_to(rate_row, (PER_TILE, LANES))
        res_rows[j] = jnp.where(same_filter, res_rep, 0.0)

    for n in range(3, 7):
        loads[n].wait()
    lane_up = iota((LANES, LANES), 1).astype(F32)
    row_up = iota((LANES, LANES), 0).astype(F32)

    def tables(j, carry):
        cols = pl.ds(pl.multiple_of(j * LANES, LANES), LANES)
        rate_wide = jnp.broadcast_to(rate_rows[j, 0:1, :], (LANES, LANES))
        rate_tall = jnp.transpose(rate_wide)
        back = (rows - 1.0) - lane_up
        weight = jnp.exp(-rate_tall * back)
        w_sum[j] = jnp.concatenate([split(weight), split(weight * back)], axis=0)
        res_wide = jnp.sum(res_rows[j], axis=0, keepdims=True)
        a_out[j] = split(res_wide * jnp.exp(-rate_wide * (row_up + 1.0)))
        mode_rate = own_filter(rate_tall)
        whole = jnp.exp(-mode_rate * float(rows))
        decay[2 * j] = whole[:8]
        decay[2 * j + 1] = whole[8:]
        d_part = (cot[:, cols].astype(F32) * gate[:, cols].astype(F32)).astype(BF16)
        dn[j] = d_part
        ahead = lane_up + 1.0
        after = jnp.exp(-rate_tall * ahead)
        both = jnp.concatenate([split(after), split(after * ahead)], axis=0)
        sums = nn(both, jnp.concatenate([d_part, d_part], axis=0))
        one, two = own_filter(sums[:LANES]), own_filter(sums[LANES:])
        for half in range(2):
            c_out[2 * j + half, 0:8] = one[8 * half : 8 * half + 8]
            c_out[2 * j + half, 8:16] = two[8 * half : 8 * half + 8]
        return carry

    lax.fori_loop(0, tiles, tables, 0)
    c_in[p_me] = c_out[p_me]
    send_plane(c_out, c_in, 1)

    wait_in(sq_in, 0)
    total_sq = sq_in[0]
    for n in range(1, groups):
        total_sq += sq_in[n]
    inverse = lax.rsqrt(total_sq / float(groups * tiles * LANES) + EPSILON)
    inverse = jnp.transpose(jnp.broadcast_to(inverse[0:1, :], (LANES, LANES)))

    def summaries(j, carry):
        cols = pl.ds(pl.multiple_of(j * LANES, LANES), LANES)
        x_part = (feat[:, cols].astype(F32) * inverse * gain[pl.ds(j, 1), :]).astype(BF16)
        xn[j] = x_part
        sums = nn(w_sum[j], jnp.concatenate([x_part, x_part], axis=0))
        one, two = own_filter(sums[:LANES]), own_filter(sums[LANES:])
        for half in range(2):
            s_out[2 * j + half, 0:8] = one[8 * half : 8 * half + 8]
            s_out[2 * j + half, 8:16] = two[8 * half : 8 * half + 8]
        return carry

    lax.fori_loop(0, tiles, summaries, 0)
    s_in[p_me] = s_out[p_me]
    send_plane(s_out, s_in, 2)

    lag = jnp.where(lane_up == 0.0, 0.0, rows - lane_up)
    lag_short = lag[:PER_TILE]
    lane_filter = iota((rows, LANES), 1) // GROUP
    short_lane, short_row = iota((8, LANES), 1), iota((8, LANES), 0)
    lane_mode = iota((MODES, LANES), 1) % MODES == iota((MODES, LANES), 0)

    def pairs(j, carry):
        x_part, d_part = xn[j], dn[j]
        lag_table = jnp.exp(-jnp.broadcast_to(rate_rows[j, 0:1, :], (LANES, LANES)) * jnp.where(row_up == 0.0, 0.0, rows - row_up))
        for f in range(PER_TILE):
            masked = jnp.where(lane_filter == f, d_part, jnp.zeros_like(d_part))
            product = nt(masked, x_part)
            total = None
            for i in range(rows // 8):
                piece = jnp.where(
                    short_lane <= short_row + 8 * i, product[8 * i : 8 * i + 8], 0.0
                )
                if i:
                    piece = pltpu.roll(piece, LANES - 8 * i, 1)
                total = piece if total is None else total + piece
            diag[f] = total
        near = None
        for u in range(8):
            piece = jnp.concatenate([diag[f, u : u + 1, :] for f in range(PER_TILE)], axis=0)
            if u:
                piece = pltpu.roll(piece, LANES - u, 1)
            near = piece if near is None else near + piece
        stacked = jnp.concatenate([near, near * lag_short], axis=0)
        local = nn(stacked, lag_table, HIGHEST)
        one = jnp.sum(jnp.where(same_filter, local[:8], 0.0), axis=0, keepdims=True)
        two = jnp.sum(jnp.where(same_filter, local[8:], 0.0), axis=0, keepdims=True)
        one = jnp.where(lane_mode, one, 0.0)
        two = jnp.where(lane_mode, two, 0.0)
        for half in range(2):
            l_out[2 * j + half, 0:8] = one[8 * half : 8 * half + 8]
            l_out[2 * j + half, 8:16] = two[8 * half : 8 * half + 8]
        return carry

    lax.fori_loop(0, tiles, pairs, 0)
    l_in[p_me] = l_out[p_me]
    send_plane(l_out, l_in, 3)

    wait_in(c_in, 1)
    wait_in(s_in, 2)
    step = decay[p_me]
    zero = jnp.zeros((8, LANES), F32)
    state, second, power = zero, zero, jnp.ones((8, LANES), F32)
    back_one, back_two, grad_one, grad_two = zero, zero, zero, zero
    for p in range(plane):
        sum_one, sum_two = s_in[p, 0:8], s_in[p, 8:16]
        cot_one, cot_two = c_in[p, 0:8], c_in[p, 8:16]
        pre_one[p] = state
        grad_one += state * cot_one
        grad_two += state * cot_two + second * cot_one
        back_one += power * cot_one
        back_two += power * (cot_two + float(rows * p) * cot_one)
        second = step * (second + float(rows) * state) + sum_two
        state = step * state + sum_one
        power = power * step
    z_out[...] = state
    z_in[z_me] = state
    send_z(z_out, z_in, 4)

    wait_in(l_in, 3)
    for p in range(plane):
        grad_one += l_in[p, 0:8]
        grad_two += l_in[p, 8:16]
    for n, value in enumerate((second, back_one, back_two, grad_one, grad_two)):
        zg_out[8 * n : 8 * n + 8] = value
    zg_in[z_me] = zg_out[...]
    send_z(zg_out, zg_in, 5)

    def inside(j, carry):
        x_part = xn[j]
        lag_table = jnp.exp(-jnp.broadcast_to(rate_rows[j, 0:1, :], (LANES, LANES)) * jnp.where(row_up == 0.0, 0.0, rows - row_up))
        filters = nt(res_rows[j], lag_table, HIGHEST)
        doubled = jnp.concatenate([x_part, x_part], axis=0)
        total = skip[pl.ds(j, 1), :] * x_part.astype(F32)
        for f in range(PER_TILE):
            first = pltpu.roll(
                jnp.broadcast_to(filters[f : f + 1], (8, LANES)), 0, 1, stride=1, stride_axis=0
            )
            pieces = []
            for i in range(rows // 8):
                piece = pltpu.roll(first, 8 * i, 1) if i else first
                pieces.append(jnp.where(short_lane <= short_row + 8 * i, piece, 0.0))
            toeplitz = split(jnp.concatenate(pieces, axis=0))
            total += jnp.where(lane_filter == f, nn(toeplitz, doubled), 0.0)
        y_local[j] = total
        return carry

    lax.fori_loop(0, tiles, inside, 0)

    wait_in(z_in, 4)
    plane_step = power
    entering = zero
    for z in range(planes - 1):
        entering = jnp.where(z_me > z, plane_step * entering + z_in[z], entering)
    power = jnp.ones((8, LANES), F32)
    for p in range(plane):
        r_out[p] = pre_one[p] + power * entering
        power = power * step
    r_in[p_me] = r_out[p_me]
    send_plane(r_out, r_in, 6)

    wait_in(zg_in, 5)
    grad_one, grad_two, state, second = zero, zero, zero, zero
    for z in range(planes):
        second_z, back_one, back_two, one, two = (zg_in[z, 8 * n : 8 * n + 8] for n in range(5))
        grad_one += one + state * back_one
        grad_two += two + state * back_two + second * back_one
        second = plane_step * (second + float(rows * plane) * state) + second_z
        state = plane_step * state + z_in[z]
    for p in range(plane):
        g_out[p, 0:8] = grad_one
        g_out[p, 8:16] = grad_two
    g_in[p_me] = g_out[p_me]
    send_plane(g_out, g_in, 7)

    wait_in(r_in, 6)
    own = iota((LANES, LANES), 1) // GROUP == iota((LANES, LANES), 0) // MODES

    def finish(j, carry):
        cols = pl.ds(pl.multiple_of(j * LANES, LANES), LANES)
        states = jnp.concatenate([r_in[2 * j], r_in[2 * j + 1]] * PER_TILE, axis=0)
        states = jnp.where(own, states, 0.0).astype(BF16)
        carried = nn(a_out[j], jnp.concatenate([states, states], axis=0))
        conv = (y_local[j] + carried).astype(BF16)
        out_ref[:, cols] = (gate[:, cols].astype(F32) * conv.astype(F32)).astype(BF16)
        return carry

    lax.fori_loop(0, tiles, finish, 0)

    wait_in(g_in, 7)
    same = same_filter.astype(F32)
    for j in range(tiles):
        part = slice(j * PER_TILE, (j + 1) * PER_TILE)
        stacked = jnp.concatenate(
            [g_in[2 * j, 0:8], g_in[2 * j + 1, 0:8], g_in[2 * j, 8:16], g_in[2 * j + 1, 8:16]],
            axis=0,
        )
        grads = nt(same, stacked, HIGHEST)
        gres_ref[part, :] = grads[:, :MODES] / float(length)
        grate_ref[part, :] = (
            -(res[part, :] * jnp.exp(lrate[part, :]) / float(length)) * grads[:, MODES:]
        )

    wait_out(sq_in, 0)
    for kind, buffer in ((1, c_in), (2, s_in), (3, l_in), (4, z_in), (5, zg_in), (6, r_in), (7, g_in)):
        wait_out(buffer, kind)


def solution(mesh):
    groups = mesh.shape["ch"]
    blocks = mesh.shape["ctx"]
    plane = 16
    planes = blocks // plane

    def local(features, norm_gain, skip_gain, gate_value, cotangent, residue, log_rate):
        rows, chans = features.shape
        tiles = chans // LANES
        filters = residue.shape[0]
        wide = lambda *shape: pltpu.VMEM(shape, F32)
        half = lambda *shape: pltpu.VMEM(shape, BF16)
        any_spec = pl.BlockSpec(memory_space=pl.ANY)
        vmem_spec = pl.BlockSpec(memory_space=pltpu.VMEM)
        return pl.pallas_call(
            functools.partial(body, plane, planes, groups, rows * blocks),
            out_shape=(
                jax.ShapeDtypeStruct((rows, chans), BF16),
                jax.ShapeDtypeStruct((filters, MODES), F32),
                jax.ShapeDtypeStruct((filters, MODES), F32),
            ),
            in_specs=[any_spec] * 7,
            out_specs=(vmem_spec,) * 3,
            scratch_shapes=[
                half(rows, chans), wide(tiles, LANES), wide(tiles, LANES), half(rows, chans),
                half(rows, chans), wide(filters, MODES), wide(filters, MODES),
                half(tiles, rows, LANES), half(tiles, rows, LANES),
                wide(tiles, 8, LANES), wide(tiles, 8, LANES),
                half(tiles, 2 * LANES, 2 * LANES), half(tiles, LANES, 2 * LANES),
                wide(plane, 8, LANES), wide(tiles, rows, LANES), wide(PER_TILE, 8, LANES),
                wide(8, LANES), wide(groups, 8, LANES),
                wide(plane, 16, LANES), wide(plane, 16, LANES),
                wide(plane, 16, LANES), wide(plane, 16, LANES),
                wide(plane, 16, LANES), wide(plane, 16, LANES),
                wide(8, LANES), wide(planes, 8, LANES),
                wide(40, LANES), wide(planes, 40, LANES),
                wide(plane, 8, LANES), wide(plane, 8, LANES),
                wide(plane, 16, LANES), wide(plane, 16, LANES),
                wide(plane, 8, LANES),
                pltpu.SemaphoreType.DMA((7,)),
                pltpu.SemaphoreType.DMA((8,)),
                pltpu.SemaphoreType.DMA((8,)),
            ],
            compiler_params=pltpu.CompilerParams(
                collective_id=0, has_side_effects=True, vmem_limit_bytes=48 * 1024 * 1024
            ),
        )(
            features,
            norm_gain.reshape(tiles, LANES),
            skip_gain.reshape(tiles, LANES),
            gate_value,
            cotangent,
            residue,
            log_rate,
        )

    in_specs = (
        P("ctx", "ch"),
        P("ch"),
        P("ch"),
        P("ctx", "ch"),
        P("ctx", "ch"),
        P("ch", None),
        P("ch", None),
    )
    out_specs = (P("ctx", "ch"), P("ch", None), P("ch", None))
    return jax.shard_map(local, mesh=mesh, in_specs=in_specs, out_specs=out_specs, check_vma=False)
```

```python
import functools

import jax
import jax.numpy as jnp
from jax import lax
from jax.experimental import pallas as pl
from jax.experimental.pallas import tpu as pltpu
from jax.sharding import PartitionSpec as P

EPSILON = 1e-06
HIGHEST = lax.Precision.HIGHEST
F32 = jnp.float32
BF16 = jnp.bfloat16
LANES = 128
MODES = 16
GROUP = 16
PER_TILE = 8
SIDE = 4
UNROLL = 8
UNROLL_PAIRS = 8
MESH = pl.DeviceIdType.MESH


def iota(shape, axis):
    return lax.broadcasted_iota(jnp.int32, shape, axis)


def nt(a, b, precision=None):
    return lax.dot_general(
        a, b, (((1,), (1,)), ((), ())), precision=precision, preferred_element_type=F32
    )


def nn(a, b, precision=None):
    return lax.dot_general(
        a, b, (((1,), (0,)), ((), ())), precision=precision, preferred_element_type=F32
    )


def split(x):
    high = x.astype(BF16)
    low = (x - high.astype(F32)).astype(BF16)
    return jnp.concatenate([high, low], axis=1)


def own_filter(values):
    lane_filter = iota((MODES, LANES), 1) // GROUP
    kept = values[:MODES]
    for f in range(1, PER_TILE):
        kept = jnp.where(lane_filter == f, values[f * MODES : (f + 1) * MODES], kept)
    return kept


def body(
    plane, planes, groups, length,
    feat_hbm, gain_hbm, skip_hbm, gate_hbm, cot_hbm, res_hbm, lrate_hbm,
    out_ref, gres_ref, grate_ref,
    feat, gain, skip, gate, cot, res, lrate,
    xn, dn, rate_rows, res_rows, w_sum, a_out, lag_exp, toeplitz, decay, powers, y_local, diag,
    sq_out, sq_in, c_out, c_in, s_out, s_in, l_out, l_in,
    zc_out, zc_in, z_out, z_in, zg_out, zg_in, r_out, r_in, g_out, g_in,
    pre_one,
    load_sem, send_sem, recv_sem, plane_sem, far_sem,
):
    rows = feat.shape[0]
    tiles = feat.shape[1] // LANES
    filters = lrate.shape[1]
    ctx, ch = lax.axis_index("ctx"), lax.axis_index("ch")
    z_me, p_me = ctx // plane, ctx % plane
    x_me, y_me = p_me // SIDE, p_me % SIDE

    loads = [
        pltpu.make_async_copy(src, dst, load_sem.at[n])
        for n, (src, dst) in enumerate(
            (
                (feat_hbm, feat), (lrate_hbm, lrate), (res_hbm, res), (gain_hbm, gain),
                (skip_hbm, skip), (cot_hbm, cot), (gate_hbm, gate),
            )
        )
    ]
    for load in loads:
        load.start()

    def at(z, x, y):
        return {"ctx": z * plane + x * SIDE + y}

    def signal(sem, device):
        pl.semaphore_signal(sem, inc=1, device_id=device, device_id_type=MESH)

    z_next, z_last = (z_me + 1) % planes, (z_me + planes - 1) % planes

    barrier = pltpu.get_barrier_semaphore()
    signal(barrier, at(z_next, x_me, y_me))
    signal(barrier, at(z_last, x_me, y_me))
    for i in (2, 1, 3):
        signal(barrier, at(z_me, (x_me + i) % SIDE, y_me))
        signal(barrier, at(z_me, x_me, (y_me + i) % SIDE))
    for i in range(1, groups):
        signal(barrier, {"ch": (ch + i) % groups})

    def send_plane(src, dst, kind):
        for i in range(1, plane):
            peer = (p_me + i) % plane
            pltpu.make_async_remote_copy(
                src_ref=src.at[peer], dst_ref=dst.at[p_me],
                send_sem=send_sem.at[kind], recv_sem=recv_sem.at[kind],
                device_id={"ctx": z_me * plane + peer}, device_id_type=MESH,
            ).start()

    def send_z(src, dst, kind):
        for i in (2, 1, 3):
            pltpu.make_async_remote_copy(
                src_ref=src, dst_ref=dst.at[z_me],
                send_sem=send_sem.at[kind], recv_sem=recv_sem.at[kind],
                device_id={"ctx": ((z_me + i) % planes) * plane + p_me}, device_id_type=MESH,
            ).start()

    def send_groups(src, dst, kind):
        for i in range(1, groups):
            pltpu.make_async_remote_copy(
                src_ref=src, dst_ref=dst.at[ch],
                send_sem=send_sem.at[kind], recv_sem=recv_sem.at[kind],
                device_id={"ch": (ch + i) % groups}, device_id_type=MESH,
            ).start()

    def wait_in(dst, kind):
        part = dst.at[pl.ds(0, dst.shape[0] - 1)]
        pltpu.make_async_copy(part, part, recv_sem.at[kind]).wait()

    def wait_out(dst, kind):
        part = dst.at[pl.ds(0, dst.shape[0] - 1)]
        pltpu.make_async_copy(part, part, send_sem.at[kind]).wait()

    loads[0].wait()
    squares = jnp.zeros((rows, LANES), F32)
    for j in range(tiles):
        part = feat[:, j * LANES : (j + 1) * LANES].astype(F32)
        squares += part * part
    sq_row = jnp.sum(jnp.transpose(squares), axis=0, keepdims=True)
    sq_out[...] = jnp.broadcast_to(sq_row, sq_out.shape)
    sq_in[ch] = sq_out[...]
    pl.semaphore_wait(barrier, (groups - 1) + 2 * (SIDE - 1) + 2)
    send_groups(sq_out, sq_in, 0)
    for i in range(1, SIDE):
        signal(plane_sem, at(z_me, (x_me + i) % SIDE, y_me))
    signal(far_sem, at(z_last, x_me, y_me))

    loads[1].wait()
    loads[2].wait()
    same_filter = iota((PER_TILE, LANES), 1) // MODES == iota((PER_TILE, LANES), 0)
    lane_mode = iota((MODES, LANES), 1) % MODES == iota((MODES, LANES), 0)
    own_lanes = (
        iota((filters, tiles * LANES), 1) // GROUP == iota((filters, tiles * LANES), 0)
    ).astype(F32)
    spread = nn(jnp.concatenate([jnp.exp(lrate[...]), res[...]], axis=0), own_lanes, HIGHEST)
    for j in range(tiles):
        rate_rep = spread[:MODES, j * LANES : (j + 1) * LANES]
        res_rep = spread[MODES:, j * LANES : (j + 1) * LANES]
        whole = jnp.exp(-rate_rep * float(rows))
        decay[2 * j] = whole[:8]
        decay[2 * j + 1] = whole[8:]
        rate_row = jnp.sum(jnp.where(lane_mode, rate_rep, 0.0), axis=0, keepdims=True)
        res_row = jnp.sum(jnp.where(lane_mode, res_rep, 0.0), axis=0, keepdims=True)
        rate_rows[j] = jnp.broadcast_to(rate_row, (PER_TILE, LANES))
        res_rows[j] = jnp.where(same_filter, res_row, 0.0)
    step = decay[p_me]
    power = jnp.ones((8, LANES), F32)
    for p in range(plane):
        powers[p] = power
        power = power * step
    plane_step = power

    for n in range(3, 7):
        loads[n].wait()
    lane_up = iota((LANES, LANES), 1).astype(F32)
    row_up = iota((LANES, LANES), 0).astype(F32)
    lag_rows = jnp.where(row_up == 0.0, 0.0, rows - row_up)

    def tables(j, carry):
        cols = pl.ds(pl.multiple_of(j * LANES, LANES), LANES)
        rate_wide = jnp.broadcast_to(rate_rows[j, 0:1, :], (LANES, LANES))
        rate_tall = jnp.transpose(rate_wide)
        d_part = (cot[:, cols].astype(F32) * gate[:, cols].astype(F32)).astype(BF16)
        dn[j] = d_part
        ahead = lane_up + 1.0
        after = jnp.exp(-rate_tall * ahead)
        both = jnp.concatenate([split(after), split(after * ahead)], axis=0)
        sums = nn(both, jnp.concatenate([d_part, d_part], axis=0))
        one, two = own_filter(sums[:LANES]), own_filter(sums[LANES:])
        for half in range(2):
            c_out[2 * j + half, 0:8] = one[8 * half : 8 * half + 8]
            c_out[2 * j + half, 8:16] = two[8 * half : 8 * half + 8]
        back = (rows - 1.0) - lane_up
        weight = jnp.exp(-rate_tall * back)
        w_sum[j] = jnp.concatenate([split(weight), split(weight * back)], axis=0)
        return carry

    lax.fori_loop(0, tiles, tables, 0, unroll=UNROLL)
    c_in[p_me] = c_out[p_me]
    pl.semaphore_wait(plane_sem, SIDE - 1)
    send_plane(c_out, c_in, 1)

    tall, wide = iota((2 * MODES // 2, LANES), 0), iota((2 * MODES // 2, LANES), 1)

    def builds(j, carry):
        rate_wide = jnp.broadcast_to(rate_rows[j, 0:1, :], (LANES, LANES))
        res_wide = jnp.sum(res_rows[j], axis=0, keepdims=True)
        leaving = split(res_wide * jnp.exp(-rate_wide * (row_up + 1.0)))
        a_out[j, :, 0 : 2 * LANES] = leaving
        a_out[j, :, 2 * LANES :] = leaving[:, :LANES]
        table = jnp.exp(-rate_wide * lag_rows)
        lag_exp[j] = table
        taps = nt(res_rows[j], table, HIGHEST)
        for f in range(PER_TILE):
            first = pltpu.roll(
                jnp.broadcast_to(taps[f : f + 1], (16, LANES)), 0, 1, stride=1, stride_axis=0
            )
            high = first.astype(BF16)
            low = (first - high.astype(F32)).astype(BF16)
            for i in range(rows // 16):
                causal = wide <= tall + 16 * i
                for side, piece in enumerate((high, low)):
                    moved = pltpu.roll(piece, 16 * i, 1) if i else piece
                    toeplitz[j, f * rows + 16 * i : f * rows + 16 * i + 16, side * LANES : (side + 1) * LANES] = (
                        jnp.where(causal, moved, jnp.zeros_like(moved))
                    )
        return carry

    lax.fori_loop(0, tiles, builds, 0, unroll=UNROLL)

    wait_in(sq_in, 0)
    total_sq = sq_in[0]
    for n in range(1, groups):
        total_sq += sq_in[n]
    inverse = lax.rsqrt(total_sq / float(groups * tiles * LANES) + EPSILON)
    inverse = jnp.transpose(jnp.broadcast_to(inverse[0:1, :], (LANES, LANES)))

    def summaries(j, carry):
        cols = pl.ds(pl.multiple_of(j * LANES, LANES), LANES)
        x_part = (feat[:, cols].astype(F32) * inverse * gain[pl.ds(j, 1), :]).astype(BF16)
        xn[j] = x_part
        sums = nn(w_sum[j], jnp.concatenate([x_part, x_part], axis=0))
        one, two = own_filter(sums[:LANES]), own_filter(sums[LANES:])
        for half in range(2):
            s_out[2 * j + half, 0:8] = one[8 * half : 8 * half + 8]
            s_out[2 * j + half, 8:16] = two[8 * half : 8 * half + 8]
        return carry

    lax.fori_loop(0, tiles, summaries, 0, unroll=UNROLL)
    s_in[p_me] = s_out[p_me]
    send_plane(s_out, s_in, 2)

    wait_in(c_in, 1)
    zero = jnp.zeros((8, LANES), F32)
    back_one, back_two = zero, zero
    for p in range(plane):
        cot_one, cot_two = c_in[p, 0:8], c_in[p, 8:16]
        back_one += powers[p] * cot_one
        back_two += powers[p] * (cot_two + float(rows * p) * cot_one)
    zc_out[0:8] = back_one
    zc_out[8:16] = back_two
    zc_in[z_me] = zc_out[...]
    pl.semaphore_wait(far_sem, 1)
    send_z(zc_out, zc_in, 3)

    lane_filter = iota((rows, LANES), 1) // GROUP
    short_lane, short_row = iota((8, LANES), 1), iota((8, LANES), 0)
    lag_short = jnp.where(short_lane == 0, 0, rows - short_lane).astype(F32)
    in_group = short_lane % GROUP

    def pairs(j, carry):
        x_part, d_part = xn[j], dn[j]
        masked = [
            jnp.where(lane_filter == f, d_part, jnp.zeros_like(d_part)) for f in range(PER_TILE)
        ]
        product = nt(jnp.concatenate(masked, axis=0), x_part)
        for f in range(PER_TILE):
            total = None
            for i in range(rows // 8):
                piece = jnp.where(
                    short_lane <= short_row + 8 * i,
                    product[f * rows + 8 * i : f * rows + 8 * i + 8],
                    0.0,
                )
                if i:
                    piece = pltpu.roll(piece, LANES - 8 * i, 1)
                total = piece if total is None else total + piece
            diag[j, 8 * f : 8 * f + 8] = total
        near = None
        for u in range(8):
            piece = diag[j, pl.ds(u, PER_TILE, stride=8), :]
            if u:
                piece = pltpu.roll(piece, LANES - u, 1)
            near = piece if near is None else near + piece
        stacked = jnp.concatenate([near, near * lag_short], axis=0)
        local = nn(stacked, lag_exp[j], HIGHEST)
        one = jnp.sum(jnp.where(same_filter, local[:8], 0.0), axis=0, keepdims=True)
        two = jnp.sum(jnp.where(same_filter, local[8:], 0.0), axis=0, keepdims=True)
        one = jnp.broadcast_to(one, (8, LANES))
        two = jnp.broadcast_to(two, (8, LANES))
        ones = (one, pltpu.roll(one, LANES - 8, 1))
        twos = (pltpu.roll(two, 8, 1), two)
        for half in range(2):
            l_out[2 * j + half] = jnp.where(
                in_group == short_row, ones[half], jnp.where(in_group == short_row + 8, twos[half], 0.0)
            )
        return carry

    lax.fori_loop(0, tiles, pairs, 0, unroll=UNROLL_PAIRS)
    l_in[p_me] = l_out[p_me]
    send_plane(l_out, l_in, 4)

    wait_in(s_in, 2)
    state = zero
    for p in range(plane):
        pre_one[p] = state
        state = step * state + s_in[p, 0:8]
    z_out[...] = state
    z_in[z_me] = state
    send_z(z_out, z_in, 5)
    second, grad_one, grad_two = zero, zero, zero
    for p in range(plane):
        before = pre_one[p]
        cot_one, cot_two = c_in[p, 0:8], c_in[p, 8:16]
        grad_one += before * cot_one
        grad_two += before * cot_two + second * cot_one
        second = step * (second + float(rows) * before) + s_in[p, 8:16]
    wait_in(zc_in, 3)
    back_one, back_two = zero, zero
    for z in range(planes - 1, 0, -1):
        later = z_me < z
        back_two = jnp.where(
            later, plane_step * (back_two + float(rows * plane) * back_one) + zc_in[z, 8:16], back_two
        )
        back_one = jnp.where(later, plane_step * back_one + zc_in[z, 0:8], back_one)
    grad_one += state * back_one
    grad_two += second * back_one + state * back_two
    first_half = in_group < 8
    packed = jnp.where(
        first_half, grad_one + pltpu.roll(grad_one, LANES - 8, 1), grad_two + pltpu.roll(grad_two, 8, 1)
    )
    wait_in(l_in, 4)
    for p in range(plane):
        packed += l_in[p]
    zg_out[...] = packed
    zg_in[z_me] = packed
    send_z(zg_out, zg_in, 6)

    def inside(j, carry):
        x_part = xn[j]
        spread_out = nn(toeplitz[j], jnp.concatenate([x_part, x_part], axis=0))
        total = spread_out[:rows]
        for f in range(1, PER_TILE):
            total = jnp.where(lane_filter == f, spread_out[f * rows : (f + 1) * rows], total)
        y_local[j] = total + skip[pl.ds(j, 1), :] * x_part.astype(F32)
        return carry

    lax.fori_loop(0, tiles, inside, 0, unroll=UNROLL)

    wait_in(z_in, 5)
    entering = zero
    for z in range(planes - 1):
        entering = jnp.where(z_me > z, plane_step * entering + z_in[z], entering)
    for p in range(plane):
        r_out[p] = pre_one[p] + powers[p] * entering
    r_in[p_me] = r_out[p_me]
    send_plane(r_out, r_in, 7)
    wait_in(zg_in, 6)
    packed = zg_in[0]
    for z in range(1, planes):
        packed += zg_in[z]
    for p in range(plane):
        g_out[p] = packed
    g_in[p_me] = packed
    send_plane(g_out, g_in, 8)

    own = iota((MODES, LANES), 1) // GROUP
    wait_in(r_in, 7)

    def finish(j, carry):
        cols = pl.ds(pl.multiple_of(j * LANES, LANES), LANES)
        states = jnp.concatenate([r_in[2 * j], r_in[2 * j + 1]], axis=0)
        high = states.astype(BF16)
        low = (states - high.astype(F32)).astype(BF16)
        high = [jnp.where(own == f, high, jnp.zeros_like(high)) for f in range(PER_TILE)]
        low = [jnp.where(own == f, low, jnp.zeros_like(low)) for f in range(PER_TILE)]
        carried = nn(a_out[j], jnp.concatenate(high + high + low, axis=0))
        conv = (y_local[j] + carried).astype(BF16)
        out_ref[:, cols] = (gate[:, cols].astype(F32) * conv.astype(F32)).astype(BF16)
        return carry

    lax.fori_loop(0, tiles, finish, 0, unroll=UNROLL)

    wait_in(g_in, 8)
    total = jnp.concatenate(
        [jnp.concatenate([g_in[2 * j], g_in[2 * j + 1]], axis=0) for j in range(tiles)], axis=1
    )
    first_half = iota(total.shape, 1) % GROUP < 8
    total = jnp.concatenate(
        [jnp.where(first_half, total, 0.0), jnp.where(first_half, 0.0, total)], axis=0
    )
    grads = nt(total, own_lanes, HIGHEST)
    gres_ref[...] = grads[:MODES] / float(length)
    grate_ref[...] = -(res[...] * jnp.exp(lrate[...]) / float(length)) * grads[MODES:]

    for kind, buffer in enumerate((sq_in, c_in, s_in, zc_in, l_in, z_in, zg_in, r_in, g_in)):
        wait_out(buffer, kind)


def hand_on(gated, grad_res, grad_rate, gated_hbm, grad_res_hbm, grad_rate_hbm, sem):
    copies = [
        pltpu.make_async_copy(src, dst, sem.at[n])
        for n, (src, dst) in enumerate(
            ((gated, gated_hbm), (grad_res, grad_res_hbm), (grad_rate, grad_rate_hbm))
        )
    ]
    for copy in copies:
        copy.start()
    for copy in copies:
        copy.wait()


def solution(mesh):
    groups = mesh.shape["ch"]
    blocks = mesh.shape["ctx"]
    plane = SIDE * SIDE
    planes = blocks // plane

    def local(features, norm_gain, skip_gain, gate_value, cotangent, residue, log_rate):
        rows, chans = features.shape
        tiles = chans // LANES
        filters = residue.shape[0]
        wide = lambda *shape: pltpu.VMEM(shape, F32)
        half = lambda *shape: pltpu.VMEM(shape, BF16)
        far_spec = pl.BlockSpec(memory_space=pltpu.HBM)
        near_spec = pl.BlockSpec(memory_space=pltpu.VMEM)
        shapes = (
            jax.ShapeDtypeStruct((rows, chans), BF16),
            jax.ShapeDtypeStruct((MODES, filters), F32),
            jax.ShapeDtypeStruct((MODES, filters), F32),
        )
        results = pl.pallas_call(
            functools.partial(body, plane, planes, groups, rows * blocks),
            out_shape=tuple(pltpu.VMEM(part.shape, part.dtype) for part in shapes),
            in_specs=[far_spec] * 7,
            out_specs=(near_spec,) * 3,
            scratch_shapes=[
                half(rows, chans), wide(tiles, LANES), wide(tiles, LANES), half(rows, chans),
                half(rows, chans), wide(MODES, filters), wide(MODES, filters),
                half(tiles, rows, LANES), half(tiles, rows, LANES),
                wide(tiles, 8, LANES), wide(tiles, 8, LANES),
                half(tiles, 2 * LANES, 2 * LANES), half(tiles, LANES, 3 * LANES),
                wide(tiles, rows, LANES), half(tiles, PER_TILE * rows, 2 * LANES),
                wide(plane, 8, LANES), wide(plane, 8, LANES), wide(tiles, rows, LANES),
                wide(tiles, 8 * PER_TILE, LANES),
                wide(8, LANES), wide(groups, 8, LANES),
                wide(plane, 16, LANES), wide(plane, 16, LANES),
                wide(plane, 16, LANES), wide(plane, 16, LANES),
                wide(plane, 8, LANES), wide(plane, 8, LANES),
                wide(16, LANES), wide(planes, 16, LANES),
                wide(8, LANES), wide(planes, 8, LANES),
                wide(8, LANES), wide(planes, 8, LANES),
                wide(plane, 8, LANES), wide(plane, 8, LANES),
                wide(plane, 8, LANES), wide(plane, 8, LANES),
                wide(plane, 8, LANES),
                pltpu.SemaphoreType.DMA((7,)),
                pltpu.SemaphoreType.DMA((9,)),
                pltpu.SemaphoreType.DMA((9,)),
                pltpu.SemaphoreType.REGULAR,
                pltpu.SemaphoreType.REGULAR,
            ],
            compiler_params=pltpu.CompilerParams(
                collective_id=0, has_side_effects=True, vmem_limit_bytes=40 * 1024 * 1024
            ),
        )(
            *(
                pltpu.with_memory_space_constraint(part, pltpu.HBM)
                for part in (
                    features,
                    norm_gain.reshape(tiles, LANES),
                    skip_gain.reshape(tiles, LANES),
                    gate_value,
                    cotangent,
                    residue.T,
                    log_rate.T,
                )
            )
        )
        gated, grad_res, grad_rate = pl.pallas_call(
            hand_on,
            out_shape=tuple(pltpu.HBM(part.shape, part.dtype) for part in shapes),
            in_specs=[near_spec] * 3,
            out_specs=(far_spec,) * 3,
            scratch_shapes=[pltpu.SemaphoreType.DMA((3,))],
        )(*(pltpu.with_memory_space_constraint(part, pltpu.VMEM) for part in results))
        return gated, grad_res.T, grad_rate.T

    in_specs = (
        P("ctx", "ch"),
        P("ch"),
        P("ch"),
        P("ctx", "ch"),
        P("ctx", "ch"),
        P("ch", None),
        P("ch", None),
    )
    out_specs = (P("ctx", "ch"), P("ch", None), P("ch", None))
    return jax.shard_map(local, mesh=mesh, in_specs=in_specs, out_specs=out_specs, check_vma=False)
```

```python
import functools

import jax
import jax.numpy as jnp
from jax import lax
from jax.experimental import pallas as pl
from jax.experimental.pallas import tpu as pltpu
from jax.sharding import PartitionSpec as P

EPSILON = 1e-06
HIGHEST = lax.Precision.HIGHEST
F32 = jnp.float32
BF16 = jnp.bfloat16
LANES = 128
MODES = 16
GROUP = 16
PER_TILE = 8
SIDE = 4
UNROLL = 8
UNROLL_PAIRS = 8
STEP = 16
CUTS = 4
MESH = pl.DeviceIdType.MESH


def iota(shape, axis):
    return lax.broadcasted_iota(jnp.int32, shape, axis)


def nt(a, b, precision=None):
    return lax.dot_general(
        a, b, (((1,), (1,)), ((), ())), precision=precision, preferred_element_type=F32
    )


def nn(a, b, precision=None):
    return lax.dot_general(
        a, b, (((1,), (0,)), ((), ())), precision=precision, preferred_element_type=F32
    )


def split(x):
    high = x.astype(BF16)
    low = (x - high.astype(F32)).astype(BF16)
    return jnp.concatenate([high, low], axis=1)


def own_filter(values):
    lane_filter = iota((MODES, LANES), 1) // GROUP
    kept = values[:MODES]
    for f in range(1, PER_TILE):
        kept = jnp.where(lane_filter == f, values[f * MODES : (f + 1) * MODES], kept)
    return kept


def body(
    plane, planes, groups, length,
    feat_hbm, gain_hbm, skip_hbm, gate_hbm, cot_hbm, res_hbm, lrate_hbm,
    out_ref, gres_ref, grate_ref,
    feat, gain, skip, gate, cot, res, lrate,
    xn, dn, rate_rows, res_rows, w_sum, a_out, lag_exp, toeplitz, decay, powers, y_local, diag,
    sq_out, sq_in, c_out, c_in, s_out, s_in, ly_out, ly_in, lx_out, lx_in, lz_out, lz_in,
    z_out, z_in, zg_out, zg_in, r_out, r_in, g_out, g_in,
    pre_one,
    load_sem, send_sem, recv_sem, plane_sem, far_sem,
):
    rows = feat.shape[0]
    tiles = feat.shape[1] // LANES
    filters = lrate.shape[1]
    ctx, ch = lax.axis_index("ctx"), lax.axis_index("ch")
    z_me, p_me = ctx // plane, ctx % plane
    x_me, y_me = p_me // SIDE, p_me % SIDE

    cut = rows // CUTS
    small = [
        pltpu.make_async_copy(src, dst, load_sem.at[n])
        for n, (src, dst) in enumerate(((lrate_hbm, lrate), (res_hbm, res), (gain_hbm, gain), (skip_hbm, skip)))
    ]
    large = [
        [
            pltpu.make_async_copy(
                src.at[pl.ds(cut * k, cut)], dst.at[pl.ds(cut * k, cut)], load_sem.at[4 + CUTS * n + k]
            )
            for k in range(CUTS)
        ]
        for n, (src, dst) in enumerate(((feat_hbm, feat), (cot_hbm, cot), (gate_hbm, gate)))
    ]
    for load in large[0] + small + large[1] + large[2]:
        load.start()

    def at(z, x, y):
        return {"ctx": z * plane + x * SIDE + y}

    def signal(sem, device):
        pl.semaphore_signal(sem, inc=1, device_id=device, device_id_type=MESH)

    z_next, z_last = (z_me + 1) % planes, (z_me + planes - 1) % planes

    barrier = pltpu.get_barrier_semaphore()
    signal(barrier, at(z_next, x_me, y_me))
    signal(barrier, at(z_last, x_me, y_me))
    for i in (2, 1, 3):
        signal(barrier, at(z_me, (x_me + i) % SIDE, y_me))
        signal(barrier, at(z_me, x_me, (y_me + i) % SIDE))
    for i in range(1, groups):
        signal(barrier, {"ch": (ch + i) % groups})

    def send_plane(src, dst, kind):
        for i in range(1, plane):
            peer = (p_me + i) % plane
            pltpu.make_async_remote_copy(
                src_ref=src.at[peer], dst_ref=dst.at[p_me],
                send_sem=send_sem.at[kind], recv_sem=recv_sem.at[kind],
                device_id={"ctx": z_me * plane + peer}, device_id_type=MESH,
            ).start()

    def send_line(src, dst, kind, slot, peer):
        for i in (2, 1, 3):
            pltpu.make_async_remote_copy(
                src_ref=src, dst_ref=dst.at[slot],
                send_sem=send_sem.at[kind], recv_sem=recv_sem.at[kind],
                device_id=peer(i), device_id_type=MESH,
            ).start()

    def send_z(src, dst, kind):
        send_line(src, dst, kind, z_me, lambda i: at((z_me + i) % planes, x_me, y_me))

    def send_groups(src, dst, kind):
        for i in range(1, groups):
            pltpu.make_async_remote_copy(
                src_ref=src, dst_ref=dst.at[ch],
                send_sem=send_sem.at[kind], recv_sem=recv_sem.at[kind],
                device_id={"ch": (ch + i) % groups}, device_id_type=MESH,
            ).start()

    def wait_in(dst, kind):
        part = dst.at[pl.ds(0, dst.shape[0] - 1)]
        pltpu.make_async_copy(part, part, recv_sem.at[kind]).wait()

    def wait_out(dst, kind):
        part = dst.at[pl.ds(0, dst.shape[0] - 1)]
        pltpu.make_async_copy(part, part, send_sem.at[kind]).wait()

    for load in large[0]:
        load.wait()
    squares = jnp.zeros((rows, LANES), F32)
    for j in range(tiles):
        part = feat[:, j * LANES : (j + 1) * LANES].astype(F32)
        squares += part * part
    sq_row = jnp.sum(jnp.transpose(squares), axis=0, keepdims=True)
    sq_out[...] = jnp.broadcast_to(sq_row, sq_out.shape)
    sq_in[ch] = sq_out[...]

    for load in small:
        load.wait()
    same_filter = iota((PER_TILE, LANES), 1) // MODES == iota((PER_TILE, LANES), 0)
    lane_mode = iota((MODES, LANES), 1) % MODES == iota((MODES, LANES), 0)
    own_lanes = (
        iota((filters, tiles * LANES), 1) // GROUP == iota((filters, tiles * LANES), 0)
    ).astype(F32)
    spread = nn(jnp.concatenate([jnp.exp(lrate[...]), res[...]], axis=0), own_lanes, HIGHEST)
    for j in range(tiles):
        rate_rep = spread[:MODES, j * LANES : (j + 1) * LANES]
        res_rep = spread[MODES:, j * LANES : (j + 1) * LANES]
        whole = jnp.exp(-rate_rep * float(rows))
        decay[2 * j] = whole[:8]
        decay[2 * j + 1] = whole[8:]
        rate_row = jnp.sum(jnp.where(lane_mode, rate_rep, 0.0), axis=0, keepdims=True)
        res_row = jnp.sum(jnp.where(lane_mode, res_rep, 0.0), axis=0, keepdims=True)
        rate_rows[j] = jnp.broadcast_to(rate_row, (PER_TILE, LANES))
        res_rows[j] = jnp.where(same_filter, res_row, 0.0)
    step = decay[p_me]
    power = jnp.ones((8, LANES), F32)
    for p in range(plane):
        powers[p] = power
        power = power * step
    plane_step = power

    for load in large[1] + large[2]:
        load.wait()
    lane_up = iota((LANES, LANES), 1).astype(F32)
    row_up = iota((LANES, LANES), 0).astype(F32)
    lag_rows = jnp.where(row_up == 0.0, 0.0, rows - row_up)

    def tables(j, carry):
        cols = pl.ds(pl.multiple_of(j * LANES, LANES), LANES)
        rate_wide = jnp.broadcast_to(rate_rows[j, 0:1, :], (LANES, LANES))
        rate_tall = jnp.transpose(rate_wide)
        d_part = (cot[:, cols].astype(F32) * gate[:, cols].astype(F32)).astype(BF16)
        dn[j] = d_part
        ahead = lane_up + 1.0
        after = jnp.exp(-rate_tall * ahead)
        both = jnp.concatenate([split(after), split(after * ahead)], axis=0)
        sums = nn(both, jnp.concatenate([d_part, d_part], axis=0))
        one, two = own_filter(sums[:LANES]), own_filter(sums[LANES:])
        for half in range(2):
            c_out[2 * j + half, 0:8] = one[8 * half : 8 * half + 8]
            c_out[2 * j + half, 8:16] = two[8 * half : 8 * half + 8]
        back = (rows - 1.0) - lane_up
        weight = jnp.exp(-rate_tall * back)
        w_sum[j] = jnp.concatenate([split(weight), split(weight * back)], axis=0)
        return carry

    lax.fori_loop(0, tiles, tables, 0, unroll=UNROLL)
    c_in[p_me] = c_out[p_me]
    pl.semaphore_wait(barrier, (groups - 1) + 2 * (SIDE - 1) + 2)
    send_groups(sq_out, sq_in, 0)
    for i in range(1, SIDE):
        signal(plane_sem, at(z_me, (x_me + i) % SIDE, y_me))
    signal(far_sem, at(z_last, x_me, y_me))


    tall, wide = iota((2 * MODES // 2, LANES), 0), iota((2 * MODES // 2, LANES), 1)

    def builds(j, carry):
        rate_wide = jnp.broadcast_to(rate_rows[j, 0:1, :], (LANES, LANES))
        res_wide = jnp.sum(res_rows[j], axis=0, keepdims=True)
        leaving = split(res_wide * jnp.exp(-rate_wide * (row_up + 1.0)))
        a_out[j, :, 0 : 2 * LANES] = leaving
        a_out[j, :, 2 * LANES :] = leaving[:, :LANES]
        table = jnp.exp(-rate_wide * lag_rows)
        lag_exp[j] = table
        taps = nt(res_rows[j], table, HIGHEST)
        for f in range(PER_TILE):
            first = pltpu.roll(
                jnp.broadcast_to(taps[f : f + 1], (16, LANES)), 0, 1, stride=1, stride_axis=0
            )
            high = first.astype(BF16)
            low = (first - high.astype(F32)).astype(BF16)
            for i in range(rows // 16):
                causal = wide <= tall + 16 * i
                for side, piece in enumerate((high, low)):
                    moved = pltpu.roll(piece, 16 * i, 1) if i else piece
                    toeplitz[j, f * rows + 16 * i : f * rows + 16 * i + 16, side * LANES : (side + 1) * LANES] = (
                        jnp.where(causal, moved, jnp.zeros_like(moved))
                    )
        return carry

    lax.fori_loop(0, tiles, builds, 0, unroll=UNROLL)

    pl.semaphore_wait(plane_sem, SIDE - 1)
    send_plane(c_out, c_in, 1)

    wait_in(sq_in, 0)
    total_sq = sq_in[0]
    for n in range(1, groups):
        total_sq += sq_in[n]
    inverse = lax.rsqrt(total_sq / float(groups * tiles * LANES) + EPSILON)
    inverse = jnp.transpose(jnp.broadcast_to(inverse[0:1, :], (LANES, LANES)))

    def summaries(j, carry):
        cols = pl.ds(pl.multiple_of(j * LANES, LANES), LANES)
        x_part = (feat[:, cols].astype(F32) * inverse * gain[pl.ds(j, 1), :]).astype(BF16)
        xn[j] = x_part
        sums = nn(w_sum[j], jnp.concatenate([x_part, x_part], axis=0))
        one, two = own_filter(sums[:LANES]), own_filter(sums[LANES:])
        for half in range(2):
            s_out[2 * j + half, 0:8] = one[8 * half : 8 * half + 8]
            s_out[2 * j + half, 8:16] = two[8 * half : 8 * half + 8]
        return carry

    lax.fori_loop(0, tiles, summaries, 0, unroll=UNROLL)
    s_in[p_me] = s_out[p_me]
    send_plane(s_out, s_in, 2)

    lane_filter = iota((rows, LANES), 1) // GROUP
    step_filter = iota((STEP, LANES), 1) // GROUP
    short_lane, short_row = iota((8, LANES), 1), iota((8, LANES), 0)
    lag_short = jnp.where(short_lane == 0, 0, rows - short_lane).astype(F32)
    pair_lane, row_step = iota((PER_TILE * STEP, LANES), 1), iota((PER_TILE * STEP, LANES), 0) % STEP
    earlier = (pair_lane <= row_step) | (pair_lane >= STEP)

    def pairs(j, carry):
        x_part, d_part = xn[j], dn[j]
        left, right = [], []
        for i in range(rows // STEP):
            d_rows = d_part[STEP * i : STEP * (i + 1)]
            left.append(
                jnp.concatenate(
                    [jnp.where(step_filter == f, d_rows, jnp.zeros_like(d_rows)) for f in range(PER_TILE)],
                    axis=0,
                )
            )
            moved = [x_part[STEP * i : STEP * (i + 1)]]
            if STEP * (i + 1) < rows:
                moved.append(jnp.zeros((rows - STEP * (i + 1), LANES), BF16))
            if i:
                moved.append(x_part[: STEP * i])
            right.append(jnp.concatenate(moved, axis=0))
        product = nt(jnp.concatenate(left, axis=1), jnp.concatenate(right, axis=1))
        diag[j] = jnp.where(earlier, product, 0.0)
        near = None
        for u in range(STEP):
            piece = diag[j, pl.ds(u, PER_TILE, stride=STEP), :]
            if u:
                piece = pltpu.roll(piece, LANES - u, 1)
            near = piece if near is None else near + piece
        stacked = jnp.concatenate([near, near * lag_short], axis=0)
        local = nn(stacked, lag_exp[j], HIGHEST)
        ly_out[pl.ds(j, 1), :] = jnp.sum(jnp.where(same_filter, local[:8], 0.0), axis=0, keepdims=True)
        ly_out[pl.ds(tiles + j, 1), :] = jnp.sum(jnp.where(same_filter, local[8:], 0.0), axis=0, keepdims=True)
        return carry

    lax.fori_loop(0, tiles, pairs, 0, unroll=UNROLL_PAIRS)
    ly_in[y_me] = ly_out[...]
    send_line(ly_out, ly_in, 3, y_me, lambda i: at(z_me, x_me, (y_me + i) % SIDE))

    wait_in(c_in, 1)
    zero = jnp.zeros((8, LANES), F32)
    back_one, back_two = zero, zero
    for p in range(plane):
        cot_one, cot_two = c_in[p, 0:8], c_in[p, 8:16]
        back_one += powers[p] * cot_one
        back_two += powers[p] * (cot_two + float(rows * p) * cot_one)
    zg_out[8:16] = back_one
    zg_out[16:24] = back_two
    pl.semaphore_wait(far_sem, 1)
    wait_in(s_in, 2)
    state = zero
    for p in range(plane):
        pre_one[p] = state
        state = step * state + s_in[p, 0:8]
    z_out[...] = state
    z_in[z_me] = state
    send_z(z_out, z_in, 6)
    second, grad_one, grad_two = zero, zero, zero
    for p in range(plane):
        before = pre_one[p]
        cot_one, cot_two = c_in[p, 0:8], c_in[p, 8:16]
        grad_one += before * cot_one
        grad_two += before * cot_two + second * cot_one
        second = step * (second + float(rows) * before) + s_in[p, 8:16]

    first_half = short_lane % GROUP < GROUP // 2

    def fold(one, two):
        return jnp.where(first_half, one + pltpu.roll(one, LANES - 8, 1), two + pltpu.roll(two, 8, 1))

    zg_out[0:8] = second
    zg_out[24:32] = fold(grad_one, grad_two)
    zg_in[z_me] = zg_out[...]
    send_z(zg_out, zg_in, 7)

    def inside(j, carry):
        x_part = xn[j]
        spread_out = nn(toeplitz[j], jnp.concatenate([x_part, x_part], axis=0))
        total = spread_out[:rows]
        for f in range(1, PER_TILE):
            total = jnp.where(lane_filter == f, spread_out[f * rows : (f + 1) * rows], total)
        y_local[j] = total + skip[pl.ds(j, 1), :] * x_part.astype(F32)
        return carry

    lax.fori_loop(0, tiles, inside, 0, unroll=UNROLL)

    wait_in(ly_in, 3)
    lx_out[...] = ((ly_in[0] + ly_in[1]) + ly_in[2]) + ly_in[3]
    lx_in[x_me] = lx_out[...]
    send_line(lx_out, lx_in, 4, x_me, lambda i: at(z_me, (x_me + i) % SIDE, y_me))

    wait_in(lx_in, 4)
    lz_out[...] = ((lx_in[0] + lx_in[1]) + lx_in[2]) + lx_in[3]
    lz_in[z_me] = lz_out[...]
    send_z(lz_out, lz_in, 5)
    wait_in(z_in, 6)
    entering = zero
    for z in range(planes - 1):
        entering = jnp.where(z_me > z, plane_step * entering + z_in[z], entering)
    for p in range(plane):
        r_out[p] = pre_one[p] + powers[p] * entering
    r_in[p_me] = r_out[p_me]
    send_plane(r_out, r_in, 8)
    wait_in(zg_in, 7)
    state, second, grad_one, grad_two, packed = zero, zero, zero, zero, zero
    for z in range(planes):
        back_one, back_two = zg_in[z, 8:16], zg_in[z, 16:24]
        grad_one += state * back_one
        grad_two += second * back_one + state * back_two
        packed += zg_in[z, 24:32]
        second = plane_step * (second + float(rows * plane) * state) + zg_in[z, 0:8]
        state = plane_step * state + z_in[z]
    packed += fold(grad_one, grad_two)
    for p in range(plane):
        g_out[p] = packed
    g_in[p_me] = packed
    send_plane(g_out, g_in, 9)

    own = iota((MODES, LANES), 1) // GROUP
    wait_in(r_in, 8)

    def finish(j, carry):
        cols = pl.ds(pl.multiple_of(j * LANES, LANES), LANES)
        states = jnp.concatenate([r_in[2 * j], r_in[2 * j + 1]], axis=0)
        high = states.astype(BF16)
        low = (states - high.astype(F32)).astype(BF16)
        high = [jnp.where(own == f, high, jnp.zeros_like(high)) for f in range(PER_TILE)]
        low = [jnp.where(own == f, low, jnp.zeros_like(low)) for f in range(PER_TILE)]
        carried = nn(a_out[j], jnp.concatenate(high + high + low, axis=0))
        conv = (y_local[j] + carried).astype(BF16)
        out_ref[:, cols] = (gate[:, cols].astype(F32) * conv.astype(F32)).astype(BF16)
        return carry

    lax.fori_loop(0, tiles, finish, 0, unroll=UNROLL)

    wait_in(lz_in, 5)
    near = ((lz_in[0] + lz_in[1]) + lz_in[2]) + lz_in[3]
    wait_in(g_in, 9)
    half_lanes = iota((MODES, LANES), 1) % GROUP < GROUP // 2
    ones, twos = [], []
    for j in range(tiles):
        part = jnp.concatenate([g_in[2 * j], g_in[2 * j + 1]], axis=0)
        one = jnp.where(lane_mode, near[j : j + 1], 0.0)
        two = jnp.where(lane_mode, near[tiles + j : tiles + j + 1], 0.0)
        ones.append(jnp.where(half_lanes, part, 0.0) + one)
        twos.append(jnp.where(half_lanes, 0.0, part) + two)
    total = jnp.concatenate([jnp.concatenate(ones, axis=1), jnp.concatenate(twos, axis=1)], axis=0)
    grads = nt(total, own_lanes, HIGHEST)
    gres_ref[...] = grads[:MODES] / float(length)
    grate_ref[...] = -(res[...] * jnp.exp(lrate[...]) / float(length)) * grads[MODES:]

    for kind, buffer in enumerate(
        (sq_in, c_in, s_in, ly_in, lx_in, lz_in, z_in, zg_in, r_in, g_in)
    ):
        wait_out(buffer, kind)


def hand_on(gated, grad_res, grad_rate, gated_hbm, grad_res_hbm, grad_rate_hbm, sem):
    cut = gated.shape[0] // CUTS
    copies = [
        pltpu.make_async_copy(gated.at[pl.ds(cut * k, cut)], gated_hbm.at[pl.ds(cut * k, cut)], sem.at[k])
        for k in range(CUTS)
    ]
    copies.append(pltpu.make_async_copy(grad_res, grad_res_hbm, sem.at[CUTS]))
    copies.append(pltpu.make_async_copy(grad_rate, grad_rate_hbm, sem.at[CUTS + 1]))
    for copy in copies:
        copy.start()
    for copy in copies:
        copy.wait()


def solution(mesh):
    groups = mesh.shape["ch"]
    blocks = mesh.shape["ctx"]
    plane = SIDE * SIDE
    planes = blocks // plane

    def local(features, norm_gain, skip_gain, gate_value, cotangent, residue, log_rate):
        rows, chans = features.shape
        tiles = chans // LANES
        filters = residue.shape[0]
        wide = lambda *shape: pltpu.VMEM(shape, F32)
        half = lambda *shape: pltpu.VMEM(shape, BF16)
        far_spec = pl.BlockSpec(memory_space=pltpu.HBM)
        near_spec = pl.BlockSpec(memory_space=pltpu.VMEM)
        shapes = (
            jax.ShapeDtypeStruct((rows, chans), BF16),
            jax.ShapeDtypeStruct((MODES, filters), F32),
            jax.ShapeDtypeStruct((MODES, filters), F32),
        )
        results = pl.pallas_call(
            functools.partial(body, plane, planes, groups, rows * blocks),
            out_shape=tuple(pltpu.VMEM(part.shape, part.dtype) for part in shapes),
            in_specs=[far_spec] * 7,
            out_specs=(near_spec,) * 3,
            scratch_shapes=[
                half(rows, chans), wide(tiles, LANES), wide(tiles, LANES), half(rows, chans),
                half(rows, chans), wide(MODES, filters), wide(MODES, filters),
                half(tiles, rows, LANES), half(tiles, rows, LANES),
                wide(tiles, 8, LANES), wide(tiles, 8, LANES),
                half(tiles, 2 * LANES, 2 * LANES), half(tiles, LANES, 3 * LANES),
                wide(tiles, rows, LANES), half(tiles, PER_TILE * rows, 2 * LANES),
                wide(plane, 8, LANES), wide(plane, 8, LANES), wide(tiles, rows, LANES),
                wide(tiles, STEP * PER_TILE, LANES),
                wide(8, LANES), wide(groups, 8, LANES),
                wide(plane, 16, LANES), wide(plane, 16, LANES),
                wide(plane, 16, LANES), wide(plane, 16, LANES),
                wide(16, LANES), wide(SIDE, 16, LANES), wide(16, LANES), wide(SIDE, 16, LANES),
                wide(16, LANES), wide(planes, 16, LANES),
                wide(8, LANES), wide(planes, 8, LANES),
                wide(32, LANES), wide(planes, 32, LANES),
                wide(plane, 8, LANES), wide(plane, 8, LANES),
                wide(plane, 8, LANES), wide(plane, 8, LANES),
                wide(plane, 8, LANES),
                pltpu.SemaphoreType.DMA((4 + 3 * CUTS,)),
                pltpu.SemaphoreType.DMA((10,)),
                pltpu.SemaphoreType.DMA((10,)),
                pltpu.SemaphoreType.REGULAR,
                pltpu.SemaphoreType.REGULAR,
            ],
            compiler_params=pltpu.CompilerParams(
                collective_id=0, has_side_effects=True, vmem_limit_bytes=40 * 1024 * 1024
            ),
        )(
            *(
                pltpu.with_memory_space_constraint(part, pltpu.HBM)
                for part in (
                    features,
                    norm_gain.reshape(tiles, LANES),
                    skip_gain.reshape(tiles, LANES),
                    gate_value,
                    cotangent,
                    residue.T,
                    log_rate.T,
                )
            )
        )
        gated, grad_res, grad_rate = pl.pallas_call(
            hand_on,
            out_shape=tuple(pltpu.HBM(part.shape, part.dtype) for part in shapes),
            in_specs=[near_spec] * 3,
            out_specs=(far_spec,) * 3,
            scratch_shapes=[pltpu.SemaphoreType.DMA((CUTS + 2,))],
        )(*(pltpu.with_memory_space_constraint(part, pltpu.VMEM) for part in results))
        return gated, grad_res.T, grad_rate.T

    in_specs = (
        P("ctx", "ch"),
        P("ch"),
        P("ch"),
        P("ctx", "ch"),
        P("ctx", "ch"),
        P("ch", None),
        P("ch", None),
    )
    out_specs = (P("ctx", "ch"), P("ch", None), P("ch", None))
    return jax.shard_map(local, mesh=mesh, in_specs=in_specs, out_specs=out_specs, check_vma=False)
```

```python
import functools

import jax
import jax.numpy as jnp
from jax import lax
from jax.experimental import pallas as pl
from jax.experimental.pallas import tpu as pltpu
from jax.sharding import PartitionSpec as P

EPSILON = 1e-06
F32 = jnp.float32
BF16 = jnp.bfloat16
LANES = 128
MODES = 16
GROUP = 16
PER_TILE = 8
SIDE = 4
UNROLL = 8
UNROLL_PAIRS = 8
STEP = 16
CUTS = 4
MESH = pl.DeviceIdType.MESH
FAR_FIRST = sorted(
    ((a, b) for a in range(SIDE) for b in range(SIDE) if a or b),
    key=lambda move: (-sum(min(m, SIDE - m) for m in move), move),
)


def iota(shape, axis):
    return lax.broadcasted_iota(jnp.int32, shape, axis)


def nt(a, b):
    return lax.dot_general(a, b, (((1,), (1,)), ((), ())), preferred_element_type=F32)


def nn(a, b):
    return lax.dot_general(a, b, (((1,), (0,)), ((), ())), preferred_element_type=F32)


def split(x):
    high = x.astype(BF16)
    low = (x - high.astype(F32)).astype(BF16)
    return jnp.concatenate([high, low], axis=1)


def thirds(x):
    high = x.astype(BF16)
    rest = x - high.astype(F32)
    middle = rest.astype(BF16)
    return jnp.concatenate([high, middle, (rest - middle.astype(F32)).astype(BF16)], axis=0)


def halves(x):
    high = x.astype(BF16)
    return jnp.concatenate([high, (x - high.astype(F32)).astype(BF16)], axis=0)


def own_filter(values):
    lane_filter = iota((MODES, LANES), 1) // GROUP
    kept = values[:MODES]
    for f in range(1, PER_TILE):
        kept = jnp.where(lane_filter == f, values[f * MODES : (f + 1) * MODES], kept)
    return kept


def body(
    plane, planes, groups, length,
    feat_hbm, gain_hbm, skip_hbm, gate_hbm, cot_hbm, res_hbm, lrate_hbm,
    out_ref, gres_ref, grate_ref,
    feat, gain, skip, gate, cot, res, lrate,
    xn, dn, rate_rows, res_rows, w_sum, a_out, lag_exp, toeplitz, decay, powers, y_local, diag,
    sq_out, sq_in, c_out, c_in, s_out, s_in, ly_out, ly_in, lx_out, lx_in, lz_out, lz_in,
    z_out, z_in, r_out, r_in, q_out, q_in,
    load_sem, send_sem, recv_sem, plane_sem, far_sem,
):
    rows = feat.shape[0]
    tiles = feat.shape[1] // LANES
    filters = lrate.shape[1]
    ctx, ch = lax.axis_index("ctx"), lax.axis_index("ch")
    z_me, p_me = ctx // plane, ctx % plane
    x_me, y_me = p_me // SIDE, p_me % SIDE

    def at(z, x, y):
        return {"ctx": z * plane + x * SIDE + y}

    def signal(sem, device):
        pl.semaphore_signal(sem, inc=1, device_id=device, device_id_type=MESH)

    z_next, z_last = (z_me + 1) % planes, (z_me + planes - 1) % planes

    chip, core = ch // 2, ch % 2
    chips = groups // 2
    far = (chips - 1) * (1 - chip // (chips // 2))
    middle = chips // 2 - chip // (chips // 2)
    near = chips * (chips - 1) // 2 - chip - far - middle
    far_groups = [2 * other + (core + k) % 2 for other in (far, middle, near) for k in (0, 1)]
    far_groups.append(2 * chip + 1 - core)

    barrier = pltpu.get_barrier_semaphore()
    for group in far_groups:
        signal(barrier, {"ch": group})
    signal(barrier, at(z_next, x_me, y_me))
    signal(barrier, at(z_last, x_me, y_me))
    for i in (2, 1, 3):
        signal(barrier, at(z_me, (x_me + i) % SIDE, y_me))
        signal(barrier, at(z_me, x_me, (y_me + i) % SIDE))

    cut = rows // CUTS
    small = [
        pltpu.make_async_copy(src, dst, load_sem.at[n])
        for n, (src, dst) in enumerate(((lrate_hbm, lrate), (res_hbm, res), (gain_hbm, gain), (skip_hbm, skip)))
    ]
    large = [
        [
            pltpu.make_async_copy(
                src.at[pl.ds(cut * k, cut)], dst.at[pl.ds(cut * k, cut)], load_sem.at[4 + CUTS * n + k]
            )
            for k in range(CUTS)
        ]
        for n, (src, dst) in enumerate(((feat_hbm, feat), (cot_hbm, cot), (gate_hbm, gate)))
    ]
    for load in large[0] + small + large[1] + large[2]:
        load.start()

    def send_plane(src, dst, kind):
        for move_x, move_y in FAR_FIRST:
            peer = (x_me + move_x) % SIDE * SIDE + (y_me + move_y) % SIDE
            pltpu.make_async_remote_copy(
                src_ref=src.at[peer], dst_ref=dst.at[p_me],
                send_sem=send_sem.at[kind], recv_sem=recv_sem.at[kind],
                device_id={"ctx": z_me * plane + peer}, device_id_type=MESH,
            ).start()

    def send_line(src, dst, kind, slot, peer):
        for i in (2, 1, 3):
            pltpu.make_async_remote_copy(
                src_ref=src, dst_ref=dst.at[slot],
                send_sem=send_sem.at[kind], recv_sem=recv_sem.at[kind],
                device_id=peer(i), device_id_type=MESH,
            ).start()

    def send_z(src, dst, kind):
        send_line(src, dst, kind, z_me, lambda i: at((z_me + i) % planes, x_me, y_me))

    def send_groups(src, dst, kind):
        for group in far_groups:
            pltpu.make_async_remote_copy(
                src_ref=src, dst_ref=dst.at[ch],
                send_sem=send_sem.at[kind], recv_sem=recv_sem.at[kind],
                device_id={"ch": group}, device_id_type=MESH,
            ).start()

    def wait_in(dst, kind):
        part = dst.at[pl.ds(0, dst.shape[0] - 1)]
        pltpu.make_async_copy(part, part, recv_sem.at[kind]).wait()

    def wait_out(dst, kind):
        part = dst.at[pl.ds(0, dst.shape[0] - 1)]
        pltpu.make_async_copy(part, part, send_sem.at[kind]).wait()

    for load in large[0]:
        load.wait()
    squares = jnp.zeros((rows, LANES), F32)
    for j in range(tiles):
        part = feat[:, j * LANES : (j + 1) * LANES].astype(F32)
        squares += part * part
    sq_row = jnp.sum(jnp.transpose(squares), axis=0, keepdims=True)
    sq_out[...] = sq_row
    sq_in[ch] = sq_out[...]
    pl.semaphore_wait(barrier, (groups - 1) + 2 * (SIDE - 1) + 2)
    send_groups(sq_out, sq_in, 0)
    for i in range(1, SIDE):
        signal(plane_sem, at(z_me, (x_me + i) % SIDE, y_me))
    signal(far_sem, at(z_last, x_me, y_me))

    for load in small:
        load.wait()
    same_filter = iota((PER_TILE, LANES), 1) // MODES == iota((PER_TILE, LANES), 0)
    lane_mode = iota((MODES, LANES), 1) % MODES == iota((MODES, LANES), 0)
    own_lanes = (
        iota((filters, tiles * LANES), 1) // GROUP == iota((filters, tiles * LANES), 0)
    ).astype(F32).astype(BF16)
    spread = nn(thirds(jnp.concatenate([jnp.exp(lrate[...]), res[...]], axis=0)), own_lanes)
    spread = spread[: 2 * MODES] + spread[2 * MODES : 4 * MODES] + spread[4 * MODES :]
    for j in range(tiles):
        rate_rep = spread[:MODES, j * LANES : (j + 1) * LANES]
        res_rep = spread[MODES:, j * LANES : (j + 1) * LANES]
        whole = jnp.exp(-rate_rep * float(rows))
        decay[2 * j] = whole[:8]
        decay[2 * j + 1] = whole[8:]
        rate_row = jnp.sum(jnp.where(lane_mode, rate_rep, 0.0), axis=0, keepdims=True)
        res_row = jnp.sum(jnp.where(lane_mode, res_rep, 0.0), axis=0, keepdims=True)
        rate_rows[j] = jnp.broadcast_to(rate_row, (PER_TILE, LANES))
        res_rows[j] = jnp.where(same_filter, res_row, 0.0)
    step = decay[p_me]
    power = jnp.ones((8, LANES), F32)
    for p in range(plane):
        powers[p] = power
        power = power * step
    plane_step = power

    for load in large[1] + large[2]:
        load.wait()
    lane_up = iota((LANES, LANES), 1).astype(F32)
    row_up = iota((LANES, LANES), 0).astype(F32)
    lag_rows = jnp.where(row_up == 0.0, 0.0, rows - row_up)

    def tables(j, carry):
        cols = pl.ds(pl.multiple_of(j * LANES, LANES), LANES)
        rate_wide = jnp.broadcast_to(rate_rows[j, 0:1, :], (LANES, LANES))
        rate_tall = jnp.transpose(rate_wide)
        d_part = (cot[:, cols].astype(F32) * gate[:, cols].astype(F32)).astype(BF16)
        dn[j] = d_part
        ahead = lane_up + 1.0
        after = jnp.exp(-rate_tall * ahead)
        both = jnp.concatenate([split(after), split(after * ahead)], axis=0)
        sums = nn(both, jnp.concatenate([d_part, d_part], axis=0))
        one, two = own_filter(sums[:LANES]), own_filter(sums[LANES:])
        for half in range(2):
            c_out[2 * j + half, 0:8] = one[8 * half : 8 * half + 8]
            c_out[2 * j + half, 8:16] = two[8 * half : 8 * half + 8]
        back = (rows - 1.0) - lane_up
        weight = jnp.exp(-rate_tall * back)
        w_sum[j] = jnp.concatenate([split(weight), split(weight * back)], axis=0)
        lag_exp[j] = halves(jnp.exp(-rate_wide * lag_rows))
        return carry

    lax.fori_loop(0, tiles, tables, 0, unroll=UNROLL)
    c_in[p_me] = c_out[p_me]

    pl.semaphore_wait(plane_sem, SIDE - 1)
    send_plane(c_out, c_in, 1)

    wait_in(sq_in, 0)
    total_sq = sq_in[0]
    for n in range(1, groups):
        total_sq += sq_in[n]
    inverse = lax.rsqrt(total_sq / float(groups * tiles * LANES) + EPSILON)
    inverse = jnp.transpose(jnp.broadcast_to(inverse, (LANES, LANES)))

    def summaries(j, carry):
        cols = pl.ds(pl.multiple_of(j * LANES, LANES), LANES)
        x_part = (feat[:, cols].astype(F32) * inverse * gain[pl.ds(j, 1), :]).astype(BF16)
        xn[j] = x_part
        sums = nn(w_sum[j], jnp.concatenate([x_part, x_part], axis=0))
        one, two = own_filter(sums[:LANES]), own_filter(sums[LANES:])
        for half in range(2):
            s_out[2 * j + half, 0:8] = one[8 * half : 8 * half + 8]
            s_out[2 * j + half, 8:16] = two[8 * half : 8 * half + 8]
        return carry

    lax.fori_loop(0, tiles, summaries, 0, unroll=UNROLL)
    s_in[p_me] = s_out[p_me]
    send_plane(s_out, s_in, 2)

    lane_filter = iota((rows, LANES), 1) // GROUP
    step_filter = iota((STEP, LANES), 1) // GROUP
    short_lane, short_row = iota((8, LANES), 1), iota((8, LANES), 0)
    lag_short = jnp.where(short_lane == 0, 0, rows - short_lane).astype(F32)
    pair_lane, row_step = iota((PER_TILE * STEP, LANES), 1), iota((PER_TILE * STEP, LANES), 0) % STEP
    earlier = (pair_lane <= row_step) | (pair_lane >= STEP)

    def pairs(j, carry):
        x_part, d_part = xn[j], dn[j]
        left, right = [], []
        for i in range(rows // STEP):
            d_rows = d_part[STEP * i : STEP * (i + 1)]
            left.append(
                jnp.concatenate(
                    [jnp.where(step_filter == f, d_rows, jnp.zeros_like(d_rows)) for f in range(PER_TILE)],
                    axis=0,
                )
            )
            moved = [x_part[STEP * i : STEP * (i + 1)]]
            if STEP * (i + 1) < rows:
                moved.append(jnp.zeros((rows - STEP * (i + 1), LANES), BF16))
            if i:
                moved.append(x_part[: STEP * i])
            right.append(jnp.concatenate(moved, axis=0))
        product = nt(jnp.concatenate(left, axis=1), jnp.concatenate(right, axis=1))
        diag[j] = jnp.where(earlier, product, 0.0)
        near = None
        for u in range(STEP):
            piece = diag[j, pl.ds(u, PER_TILE, stride=STEP), :]
            if u:
                piece = pltpu.roll(piece, LANES - u, 1)
            near = piece if near is None else near + piece
        stacked = jnp.concatenate([near, near * lag_short], axis=0)
        stacked = halves(stacked)
        local = nn(stacked, lag_exp[j, :LANES])
        local = local[:16] + local[16:] + nn(stacked[:16], lag_exp[j, LANES:])
        ly_out[pl.ds(j, 1), :] = jnp.sum(jnp.where(same_filter, local[:8], 0.0), axis=0, keepdims=True)
        ly_out[pl.ds(tiles + j, 1), :] = jnp.sum(jnp.where(same_filter, local[8:], 0.0), axis=0, keepdims=True)
        return carry

    lax.fori_loop(0, tiles, pairs, 0, unroll=UNROLL_PAIRS)
    ly_in[y_me] = ly_out[...]
    send_line(ly_out, ly_in, 3, y_me, lambda i: at(z_me, x_me, (y_me + i) % SIDE))

    wait_in(c_in, 1)
    zero = jnp.zeros((8, LANES), F32)
    back_one, back_two = zero, zero
    for p in range(plane):
        cot_one, cot_two = c_in[p, 0:8], c_in[p, 8:16]
        back_one += powers[p] * cot_one
        back_two += powers[p] * (cot_two + float(rows * p) * cot_one)
    z_out[8:16] = back_one
    z_out[16:24] = back_two
    pl.semaphore_wait(far_sem, 1)

    first_half = short_lane % GROUP < GROUP // 2

    def fold(one, two):
        return jnp.where(first_half, one + pltpu.roll(one, LANES - 8, 1), two + pltpu.roll(two, 8, 1))

    wait_in(s_in, 2)
    state, second, grad_one, grad_two = zero, zero, zero, zero
    for p in range(plane):
        cot_one, cot_two = c_in[p, 0:8], c_in[p, 8:16]
        q_out[p] = state
        grad_one += state * cot_one
        grad_two += state * cot_two + second * cot_one
        second = step * (second + float(rows) * state) + s_in[p, 8:16]
        state = step * state + s_in[p, 0:8]
    z_out[0:8] = second
    z_out[24:32] = fold(grad_one, grad_two)
    z_out[32:40] = state
    z_in[z_me] = z_out[...]
    send_z(z_out, z_in, 6)
    q_in[p_me] = q_out[p_me]
    send_plane(q_out, q_in, 8)

    wait_in(ly_in, 3)
    lx_out[...] = ((ly_in[0] + ly_in[1]) + ly_in[2]) + ly_in[3]
    lx_in[x_me] = lx_out[...]
    send_line(lx_out, lx_in, 4, x_me, lambda i: at(z_me, (x_me + i) % SIDE, y_me))

    tall, wide = iota((2 * MODES // 2, LANES), 0), iota((2 * MODES // 2, LANES), 1)

    def builds(j, carry):
        rate_wide = jnp.broadcast_to(rate_rows[j, 0:1, :], (LANES, LANES))
        res_wide = jnp.sum(res_rows[j], axis=0, keepdims=True)
        leaving = split(res_wide * jnp.exp(-rate_wide * (row_up + 1.0)))
        a_out[j, :, 0 : 2 * LANES] = leaving
        a_out[j, :, 2 * LANES :] = leaving[:, :LANES]
        table = lag_exp[j]
        left = halves(res_rows[j])
        taps = nt(left, table[:LANES])
        taps = taps[:PER_TILE] + taps[PER_TILE:] + nt(left, table[LANES:])[:PER_TILE]
        for f in range(PER_TILE):
            first = pltpu.roll(
                jnp.broadcast_to(taps[f : f + 1], (16, LANES)), 0, 1, stride=1, stride_axis=0
            )
            high = first.astype(BF16)
            low = (first - high.astype(F32)).astype(BF16)
            for i in range(rows // 16):
                causal = wide <= tall + 16 * i
                for side, piece in enumerate((high, low)):
                    moved = pltpu.roll(piece, 16 * i, 1) if i else piece
                    toeplitz[j, f * rows + 16 * i : f * rows + 16 * i + 16, side * LANES : (side + 1) * LANES] = (
                        jnp.where(causal, moved, jnp.zeros_like(moved))
                    )
        return carry

    lax.fori_loop(0, tiles, builds, 0, unroll=UNROLL)

    def inside(j, carry):
        x_part = xn[j]
        spread_out = nn(toeplitz[j], jnp.concatenate([x_part, x_part], axis=0))
        total = spread_out[:rows]
        for f in range(1, PER_TILE):
            total = jnp.where(lane_filter == f, spread_out[f * rows : (f + 1) * rows], total)
        y_local[j] = total + skip[pl.ds(j, 1), :] * x_part.astype(F32)
        return carry

    lax.fori_loop(0, tiles, inside, 0, unroll=UNROLL)

    own = iota((MODES, LANES), 1) // GROUP

    def carry_in(source, j, carry):
        states = jnp.concatenate([source[2 * j, 0:8], source[2 * j + 1, 0:8]], axis=0)
        high = states.astype(BF16)
        low = (states - high.astype(F32)).astype(BF16)
        high = [jnp.where(own == f, high, jnp.zeros_like(high)) for f in range(PER_TILE)]
        low = [jnp.where(own == f, low, jnp.zeros_like(low)) for f in range(PER_TILE)]
        y_local[j] += nn(a_out[j], jnp.concatenate(high + high + low, axis=0))
        return carry

    def finish(j, carry):
        cols = pl.ds(pl.multiple_of(j * LANES, LANES), LANES)
        conv = y_local[j].astype(BF16)
        out_ref[:, cols] = (gate[:, cols].astype(F32) * conv.astype(F32)).astype(BF16)
        return carry

    wait_in(lx_in, 4)
    lz_out[...] = ((lx_in[0] + lx_in[1]) + lx_in[2]) + lx_in[3]
    lz_in[z_me] = lz_out[...]
    send_z(lz_out, lz_in, 5)
    wait_in(q_in, 8)
    lax.fori_loop(0, tiles, functools.partial(carry_in, q_in), 0, unroll=UNROLL)

    @pl.when(z_me == 0)
    def first_plane():
        lax.fori_loop(0, tiles, finish, 0, unroll=UNROLL)

    wait_in(z_in, 6)
    entering = zero
    state, second, grad_one, grad_two, packed = zero, zero, zero, zero, zero
    for z in range(planes):
        back_one, back_two, total_one = z_in[z, 8:16], z_in[z, 16:24], z_in[z, 32:40]
        entering = jnp.where(z_me == z, state, entering)
        grad_one += state * back_one
        grad_two += second * back_one + state * back_two
        packed += z_in[z, 24:32]
        second = plane_step * (second + float(rows * plane) * state) + z_in[z, 0:8]
        state = plane_step * state + total_one
    packed += fold(grad_one, grad_two)
    for p in range(plane):
        r_out[p, 0:8] = powers[p] * entering
        r_out[p, 8:16] = packed
    r_in[p_me] = r_out[p_me]
    send_plane(r_out, r_in, 7)

    wait_in(r_in, 7)

    @pl.when(z_me > 0)
    def from_other_planes():
        lax.fori_loop(0, tiles, functools.partial(carry_in, r_in), 0, unroll=UNROLL)
        lax.fori_loop(0, tiles, finish, 0, unroll=UNROLL)

    wait_in(lz_in, 5)
    near = ((lz_in[0] + lz_in[1]) + lz_in[2]) + lz_in[3]
    half_lanes = iota((MODES, LANES), 1) % GROUP < GROUP // 2
    ones, twos = [], []
    for j in range(tiles):
        part = jnp.concatenate([r_in[2 * j, 8:16], r_in[2 * j + 1, 8:16]], axis=0)
        one = jnp.where(lane_mode, near[j : j + 1], 0.0)
        two = jnp.where(lane_mode, near[tiles + j : tiles + j + 1], 0.0)
        ones.append(jnp.where(half_lanes, part, 0.0) + one)
        twos.append(jnp.where(half_lanes, 0.0, part) + two)
    total = jnp.concatenate([jnp.concatenate(ones, axis=1), jnp.concatenate(twos, axis=1)], axis=0)
    grads = nt(thirds(total), own_lanes)
    grads = grads[: 2 * MODES] + grads[2 * MODES : 4 * MODES] + grads[4 * MODES :]
    gres_ref[...] = grads[:MODES] / float(length)
    grate_ref[...] = -(res[...] * jnp.exp(lrate[...]) / float(length)) * grads[MODES:]

    for kind, buffer in enumerate(
        (sq_in, c_in, s_in, ly_in, lx_in, lz_in, z_in, r_in, q_in)
    ):
        wait_out(buffer, kind)


def hand_on(gated, grad_res, grad_rate, gated_hbm, grad_res_hbm, grad_rate_hbm, sem):
    cut = gated.shape[0] // CUTS
    copies = [
        pltpu.make_async_copy(gated.at[pl.ds(cut * k, cut)], gated_hbm.at[pl.ds(cut * k, cut)], sem.at[k])
        for k in range(CUTS)
    ]
    copies.append(pltpu.make_async_copy(grad_res, grad_res_hbm, sem.at[CUTS]))
    copies.append(pltpu.make_async_copy(grad_rate, grad_rate_hbm, sem.at[CUTS + 1]))
    for copy in copies:
        copy.start()
    for copy in copies:
        copy.wait()


def solution(mesh):
    groups = mesh.shape["ch"]
    blocks = mesh.shape["ctx"]
    plane = SIDE * SIDE
    planes = blocks // plane

    def local(features, norm_gain, skip_gain, gate_value, cotangent, residue, log_rate):
        rows, chans = features.shape
        tiles = chans // LANES
        filters = residue.shape[0]
        wide = lambda *shape: pltpu.VMEM(shape, F32)
        half = lambda *shape: pltpu.VMEM(shape, BF16)
        far_spec = pl.BlockSpec(memory_space=pltpu.HBM)
        near_spec = pl.BlockSpec(memory_space=pltpu.VMEM)
        shapes = (
            jax.ShapeDtypeStruct((rows, chans), BF16),
            jax.ShapeDtypeStruct((MODES, filters), F32),
            jax.ShapeDtypeStruct((MODES, filters), F32),
        )
        results = pl.pallas_call(
            functools.partial(body, plane, planes, groups, rows * blocks),
            out_shape=tuple(pltpu.VMEM(part.shape, part.dtype) for part in shapes),
            in_specs=[far_spec] * 7,
            out_specs=(near_spec,) * 3,
            scratch_shapes=[
                half(rows, chans), wide(tiles, LANES), wide(tiles, LANES), half(rows, chans),
                half(rows, chans), wide(MODES, filters), wide(MODES, filters),
                half(tiles, rows, LANES), half(tiles, rows, LANES),
                wide(tiles, 8, LANES), wide(tiles, 8, LANES),
                half(tiles, 2 * LANES, 2 * LANES), half(tiles, LANES, 3 * LANES),
                half(tiles, 2 * rows, LANES), half(tiles, PER_TILE * rows, 2 * LANES),
                wide(plane, 8, LANES), wide(plane, 8, LANES), wide(tiles, rows, LANES),
                wide(tiles, STEP * PER_TILE, LANES),
                wide(1, LANES), wide(groups, 1, LANES),
                wide(plane, 16, LANES), wide(plane, 16, LANES),
                wide(plane, 16, LANES), wide(plane, 16, LANES),
                wide(16, LANES), wide(SIDE, 16, LANES), wide(16, LANES), wide(SIDE, 16, LANES),
                wide(16, LANES), wide(planes, 16, LANES),
                wide(40, LANES), wide(planes, 40, LANES),
                wide(plane, 16, LANES), wide(plane, 16, LANES),
                wide(plane, 8, LANES), wide(plane, 8, LANES),
                pltpu.SemaphoreType.DMA((4 + 3 * CUTS,)),
                pltpu.SemaphoreType.DMA((9,)),
                pltpu.SemaphoreType.DMA((9,)),
                pltpu.SemaphoreType.REGULAR,
                pltpu.SemaphoreType.REGULAR,
            ],
            compiler_params=pltpu.CompilerParams(
                collective_id=0, has_side_effects=True, vmem_limit_bytes=40 * 1024 * 1024
            ),
        )(
            *(
                pltpu.with_memory_space_constraint(part, pltpu.HBM)
                for part in (
                    features,
                    norm_gain.reshape(tiles, LANES),
                    skip_gain.reshape(tiles, LANES),
                    gate_value,
                    cotangent,
                    residue.T,
                    log_rate.T,
                )
            )
        )
        gated, grad_res, grad_rate = pl.pallas_call(
            hand_on,
            out_shape=tuple(pltpu.HBM(part.shape, part.dtype) for part in shapes),
            in_specs=[near_spec] * 3,
            out_specs=(far_spec,) * 3,
            scratch_shapes=[pltpu.SemaphoreType.DMA((CUTS + 2,))],
        )(*(pltpu.with_memory_space_constraint(part, pltpu.VMEM) for part in results))
        return gated, grad_res.T, grad_rate.T

    in_specs = (
        P("ctx", "ch"),
        P("ch"),
        P("ch"),
        P("ctx", "ch"),
        P("ctx", "ch"),
        P("ch", None),
        P("ch", None),
    )
    out_specs = (P("ctx", "ch"), P("ch", None), P("ch", None))
    return jax.shard_map(local, mesh=mesh, in_specs=in_specs, out_specs=out_specs, check_vma=False)
```

```python
import functools

import jax
import jax.numpy as jnp
from jax import lax
from jax.experimental import pallas as pl
from jax.experimental.pallas import tpu as pltpu
from jax.sharding import PartitionSpec as P

EPSILON = 1e-06
F32 = jnp.float32
BF16 = jnp.bfloat16
LANES = 128
MODES = 16
GROUP = 16
PER_TILE = 8
SIDE = 4
UNROLL = 8
UNROLL_PAIRS = 8
STEP = 16
CUTS = 4
MESH = pl.DeviceIdType.MESH
FAR_FIRST = sorted(
    ((a, b) for a in range(SIDE) for b in range(SIDE) if a or b),
    key=lambda move: (-sum(min(m, SIDE - m) for m in move), move),
)


def iota(shape, axis):
    return lax.broadcasted_iota(jnp.int32, shape, axis)


def nt(a, b):
    return lax.dot_general(a, b, (((1,), (1,)), ((), ())), preferred_element_type=F32)


def nn(a, b):
    return lax.dot_general(a, b, (((1,), (0,)), ((), ())), preferred_element_type=F32)


def split(x):
    high = x.astype(BF16)
    low = (x - high.astype(F32)).astype(BF16)
    return jnp.concatenate([high, low], axis=1)


def thirds(x):
    high = x.astype(BF16)
    rest = x - high.astype(F32)
    middle = rest.astype(BF16)
    return jnp.concatenate([high, middle, (rest - middle.astype(F32)).astype(BF16)], axis=0)


def halves(x):
    high = x.astype(BF16)
    return jnp.concatenate([high, (x - high.astype(F32)).astype(BF16)], axis=0)


def own_filter(values):
    lane_filter = iota((MODES, LANES), 1) // GROUP
    kept = values[:MODES]
    for f in range(1, PER_TILE):
        kept = jnp.where(lane_filter == f, values[f * MODES : (f + 1) * MODES], kept)
    return kept


def body(
    plane, planes, groups, length,
    feat_hbm, gain_hbm, skip_hbm, gate_hbm, cot_hbm, res_hbm, lrate_hbm,
    out_ref, gres_ref, grate_ref,
    feat, gain, skip, gate, cot, res, lrate,
    xn, dn, rate_rows, res_rows, w_sum, a_out, lag_exp, toeplitz, decay, powers, y_local, diag,
    sq_out, sq_in, c_out, c_in, s_out, s_in, ly_out, ly_in, lx_out, lx_in, lz_out, lz_in,
    z_out, z_in, r_out, r_in, q_out, q_in,
    load_sem, send_sem, recv_sem, plane_sem, far_sem,
):
    rows = feat.shape[0]
    tiles = feat.shape[1] // LANES
    filters = lrate.shape[1]
    ctx, ch = lax.axis_index("ctx"), lax.axis_index("ch")
    z_me, p_me = ctx // plane, ctx % plane
    x_me, y_me = p_me // SIDE, p_me % SIDE

    def at(z, x, y):
        return {"ctx": z * plane + x * SIDE + y}

    def signal(sem, device):
        pl.semaphore_signal(sem, inc=1, device_id=device, device_id_type=MESH)

    z_next, z_last = (z_me + 1) % planes, (z_me + planes - 1) % planes

    chip, core = ch // 2, ch % 2
    chips = groups // 2
    far = (chips - 1) * (1 - chip // (chips // 2))
    middle = chips // 2 - chip // (chips // 2)
    near = chips * (chips - 1) // 2 - chip - far - middle
    far_groups = [2 * other + (core + k) % 2 for other in (far, middle, near) for k in (0, 1)]
    far_groups.append(2 * chip + 1 - core)

    barrier = pltpu.get_barrier_semaphore()
    signal(barrier, at(z_next, x_me, y_me))
    signal(barrier, at(z_last, x_me, y_me))
    for group in far_groups:
        signal(barrier, {"ch": group})
    for i in (2, 1, 3):
        signal(barrier, at(z_me, (x_me + i) % SIDE, y_me))
        signal(barrier, at(z_me, x_me, (y_me + i) % SIDE))

    cut = rows // CUTS
    small = [
        pltpu.make_async_copy(src, dst, load_sem.at[n])
        for n, (src, dst) in enumerate(((lrate_hbm, lrate), (res_hbm, res), (gain_hbm, gain), (skip_hbm, skip)))
    ]
    large = [
        [
            pltpu.make_async_copy(
                src.at[pl.ds(cut * k, cut)], dst.at[pl.ds(cut * k, cut)], load_sem.at[4 + CUTS * n + k]
            )
            for k in range(CUTS)
        ]
        for n, (src, dst) in enumerate(((feat_hbm, feat), (cot_hbm, cot), (gate_hbm, gate)))
    ]
    for load in large[0] + small + large[1] + large[2]:
        load.start()

    def send_plane(src, dst, kind):
        for move_x, move_y in FAR_FIRST:
            peer = (x_me + move_x) % SIDE * SIDE + (y_me + move_y) % SIDE
            pltpu.make_async_remote_copy(
                src_ref=src.at[peer], dst_ref=dst.at[p_me],
                send_sem=send_sem.at[kind], recv_sem=recv_sem.at[kind],
                device_id={"ctx": z_me * plane + peer}, device_id_type=MESH,
            ).start()

    def send_line(src, dst, kind, slot, peer):
        for i in (2, 1, 3):
            pltpu.make_async_remote_copy(
                src_ref=src, dst_ref=dst.at[slot],
                send_sem=send_sem.at[kind], recv_sem=recv_sem.at[kind],
                device_id=peer(i), device_id_type=MESH,
            ).start()

    def send_z(src, dst, kind):
        send_line(src, dst, kind, z_me, lambda i: at((z_me + i) % planes, x_me, y_me))

    def send_groups(src, dst, kind):
        for group in far_groups:
            pltpu.make_async_remote_copy(
                src_ref=src, dst_ref=dst.at[ch],
                send_sem=send_sem.at[kind], recv_sem=recv_sem.at[kind],
                device_id={"ch": group}, device_id_type=MESH,
            ).start()

    def wait_in(dst, kind):
        part = dst.at[pl.ds(0, dst.shape[0] - 1)]
        pltpu.make_async_copy(part, part, recv_sem.at[kind]).wait()

    def wait_out(dst, kind):
        part = dst.at[pl.ds(0, dst.shape[0] - 1)]
        pltpu.make_async_copy(part, part, send_sem.at[kind]).wait()

    for load in large[0]:
        load.wait()
    squares = jnp.zeros((rows, LANES), F32)
    for j in range(tiles):
        part = feat[:, j * LANES : (j + 1) * LANES].astype(F32)
        squares += part * part
    sq_row = jnp.sum(jnp.transpose(squares), axis=0, keepdims=True)
    sq_out[...] = sq_row
    sq_in[ch] = sq_out[...]
    pl.semaphore_wait(barrier, (groups - 1) + 2 * (SIDE - 1) + 2)
    send_groups(sq_out, sq_in, 0)
    for i in range(1, SIDE):
        signal(plane_sem, at(z_me, (x_me + i) % SIDE, y_me))
    signal(far_sem, at(z_last, x_me, y_me))

    for load in small:
        load.wait()
    same_filter = iota((PER_TILE, LANES), 1) // MODES == iota((PER_TILE, LANES), 0)
    lane_mode = iota((MODES, LANES), 1) % MODES == iota((MODES, LANES), 0)
    own_lanes = (
        iota((filters, tiles * LANES), 1) // GROUP == iota((filters, tiles * LANES), 0)
    ).astype(F32).astype(BF16)
    spread = nn(thirds(jnp.concatenate([jnp.exp(lrate[...]), res[...]], axis=0)), own_lanes)
    spread = spread[: 2 * MODES] + spread[2 * MODES : 4 * MODES] + spread[4 * MODES :]
    for j in range(tiles):
        rate_rep = spread[:MODES, j * LANES : (j + 1) * LANES]
        res_rep = spread[MODES:, j * LANES : (j + 1) * LANES]
        whole = jnp.exp(-rate_rep * float(rows))
        decay[2 * j] = whole[:8]
        decay[2 * j + 1] = whole[8:]
        rate_row = jnp.sum(jnp.where(lane_mode, rate_rep, 0.0), axis=0, keepdims=True)
        res_row = jnp.sum(jnp.where(lane_mode, res_rep, 0.0), axis=0, keepdims=True)
        rate_rows[j] = jnp.broadcast_to(rate_row, (PER_TILE, LANES))
        res_rows[j] = jnp.where(same_filter, res_row, 0.0)
    step = decay[p_me]
    power = jnp.ones((8, LANES), F32)
    for p in range(plane):
        powers[p] = power
        power = power * step
    plane_step = power

    for load in large[1] + large[2]:
        load.wait()
    lane_up = iota((LANES, LANES), 1).astype(F32)
    row_up = iota((LANES, LANES), 0).astype(F32)
    lag_rows = jnp.where(row_up == 0.0, 0.0, rows - row_up)

    def tables(j, carry):
        cols = pl.ds(pl.multiple_of(j * LANES, LANES), LANES)
        rate_wide = jnp.broadcast_to(rate_rows[j, 0:1, :], (LANES, LANES))
        rate_tall = jnp.transpose(rate_wide)
        d_part = (cot[:, cols].astype(F32) * gate[:, cols].astype(F32)).astype(BF16)
        dn[j] = d_part
        ahead = lane_up + 1.0
        after = jnp.exp(-rate_tall * ahead)
        both = jnp.concatenate([split(after), split(after * ahead)], axis=0)
        sums = nn(both, jnp.concatenate([d_part, d_part], axis=0))
        one, two = own_filter(sums[:LANES]), own_filter(sums[LANES:])
        for half in range(2):
            c_out[2 * j + half, 0:8] = one[8 * half : 8 * half + 8]
            c_out[2 * j + half, 8:16] = two[8 * half : 8 * half + 8]
        back = (rows - 1.0) - lane_up
        weight = jnp.exp(-rate_tall * back)
        w_sum[j] = jnp.concatenate([split(weight), split(weight * back)], axis=0)
        lag_exp[j] = halves(jnp.exp(-rate_wide * lag_rows))
        return carry

    lax.fori_loop(0, tiles, tables, 0, unroll=UNROLL)
    c_in[p_me] = c_out[p_me]

    pl.semaphore_wait(plane_sem, SIDE - 1)
    send_plane(c_out, c_in, 1)

    wait_in(sq_in, 0)
    total_sq = sq_in[0]
    for n in range(1, groups):
        total_sq += sq_in[n]
    inverse = lax.rsqrt(total_sq / float(groups * tiles * LANES) + EPSILON)
    inverse = jnp.transpose(jnp.broadcast_to(inverse, (LANES, LANES)))

    def summaries(j, carry):
        cols = pl.ds(pl.multiple_of(j * LANES, LANES), LANES)
        x_part = (feat[:, cols].astype(F32) * inverse * gain[pl.ds(j, 1), :]).astype(BF16)
        xn[j] = x_part
        sums = nn(w_sum[j], jnp.concatenate([x_part, x_part], axis=0))
        one, two = own_filter(sums[:LANES]), own_filter(sums[LANES:])
        for half in range(2):
            s_out[2 * j + half, 0:8] = one[8 * half : 8 * half + 8]
            s_out[2 * j + half, 8:16] = two[8 * half : 8 * half + 8]
        return carry

    lax.fori_loop(0, tiles, summaries, 0, unroll=UNROLL)
    s_in[p_me] = s_out[p_me]
    send_plane(s_out, s_in, 2)

    lane_filter = iota((rows, LANES), 1) // GROUP
    step_filter = iota((STEP, LANES), 1) // GROUP
    short_lane, short_row = iota((8, LANES), 1), iota((8, LANES), 0)
    lag_short = jnp.where(short_lane == 0, 0, rows - short_lane).astype(F32)
    pair_lane, row_step = iota((PER_TILE * STEP, LANES), 1), iota((PER_TILE * STEP, LANES), 0) % STEP
    earlier = (pair_lane <= row_step) | (pair_lane >= STEP)

    def pairs(j, carry):
        x_part, d_part = xn[j], dn[j]
        left, right = [], []
        for i in range(rows // STEP):
            d_rows = d_part[STEP * i : STEP * (i + 1)]
            left.append(
                jnp.concatenate(
                    [jnp.where(step_filter == f, d_rows, jnp.zeros_like(d_rows)) for f in range(PER_TILE)],
                    axis=0,
                )
            )
            moved = [x_part[STEP * i : STEP * (i + 1)]]
            if STEP * (i + 1) < rows:
                moved.append(jnp.zeros((rows - STEP * (i + 1), LANES), BF16))
            if i:
                moved.append(x_part[: STEP * i])
            right.append(jnp.concatenate(moved, axis=0))
        product = nt(jnp.concatenate(left, axis=1), jnp.concatenate(right, axis=1))
        diag[j] = jnp.where(earlier, product, 0.0)
        near = None
        for u in range(STEP):
            piece = diag[j, pl.ds(u, PER_TILE, stride=STEP), :]
            if u:
                piece = pltpu.roll(piece, LANES - u, 1)
            near = piece if near is None else near + piece
        stacked = jnp.concatenate([near, near * lag_short], axis=0)
        stacked = halves(stacked)
        local = nn(stacked, lag_exp[j, :LANES])
        local = local[:16] + local[16:] + nn(stacked[:16], lag_exp[j, LANES:])
        ly_out[pl.ds(j, 1), :] = jnp.sum(jnp.where(same_filter, local[:8], 0.0), axis=0, keepdims=True)
        ly_out[pl.ds(tiles + j, 1), :] = jnp.sum(jnp.where(same_filter, local[8:], 0.0), axis=0, keepdims=True)
        return carry

    lax.fori_loop(0, tiles, pairs, 0, unroll=UNROLL_PAIRS)
    ly_in[y_me] = ly_out[...]
    send_line(ly_out, ly_in, 3, y_me, lambda i: at(z_me, x_me, (y_me + i) % SIDE))

    wait_in(c_in, 1)
    zero = jnp.zeros((8, LANES), F32)
    back_one, back_two = zero, zero
    for p in range(plane):
        cot_one, cot_two = c_in[p, 0:8], c_in[p, 8:16]
        back_one += powers[p] * cot_one
        back_two += powers[p] * (cot_two + float(rows * p) * cot_one)
    z_out[8:16] = back_one
    z_out[16:24] = back_two
    pl.semaphore_wait(far_sem, 1)

    first_half = short_lane % GROUP < GROUP // 2

    def fold(one, two):
        return jnp.where(first_half, one + pltpu.roll(one, LANES - 8, 1), two + pltpu.roll(two, 8, 1))

    wait_in(s_in, 2)
    state, second, grad_one, grad_two = zero, zero, zero, zero
    for p in range(plane):
        cot_one, cot_two = c_in[p, 0:8], c_in[p, 8:16]
        q_out[p] = state
        grad_one += state * cot_one
        grad_two += state * cot_two + second * cot_one
        second = step * (second + float(rows) * state) + s_in[p, 8:16]
        state = step * state + s_in[p, 0:8]
    z_out[0:8] = second
    z_out[24:32] = fold(grad_one, grad_two)
    z_out[32:40] = state
    z_in[z_me] = z_out[...]
    send_z(z_out, z_in, 6)
    q_in[p_me] = q_out[p_me]
    send_plane(q_out, q_in, 8)

    wait_in(ly_in, 3)
    lx_out[...] = ((ly_in[0] + ly_in[1]) + ly_in[2]) + ly_in[3]
    lx_in[x_me] = lx_out[...]
    send_line(lx_out, lx_in, 4, x_me, lambda i: at(z_me, (x_me + i) % SIDE, y_me))

    tall, wide = iota((2 * MODES // 2, LANES), 0), iota((2 * MODES // 2, LANES), 1)

    def builds(j, carry):
        rate_wide = jnp.broadcast_to(rate_rows[j, 0:1, :], (LANES, LANES))
        res_wide = jnp.sum(res_rows[j], axis=0, keepdims=True)
        leaving = split(res_wide * jnp.exp(-rate_wide * (row_up + 1.0)))
        a_out[j, :, 0 : 2 * LANES] = leaving
        a_out[j, :, 2 * LANES :] = leaving[:, :LANES]
        table = lag_exp[j]
        left = halves(res_rows[j])
        taps = nt(left, table[:LANES])
        taps = taps[:PER_TILE] + taps[PER_TILE:] + nt(left, table[LANES:])[:PER_TILE]
        for f in range(PER_TILE):
            first = pltpu.roll(
                jnp.broadcast_to(taps[f : f + 1], (16, LANES)), 0, 1, stride=1, stride_axis=0
            )
            high = first.astype(BF16)
            low = (first - high.astype(F32)).astype(BF16)
            for i in range(rows // 16):
                causal = wide <= tall + 16 * i
                for side, piece in enumerate((high, low)):
                    moved = pltpu.roll(piece, 16 * i, 1) if i else piece
                    toeplitz[j, f * rows + 16 * i : f * rows + 16 * i + 16, side * LANES : (side + 1) * LANES] = (
                        jnp.where(causal, moved, jnp.zeros_like(moved))
                    )
        return carry

    lax.fori_loop(0, tiles, builds, 0, unroll=UNROLL)

    def inside(j, carry):
        x_part = xn[j]
        spread_out = nn(toeplitz[j], jnp.concatenate([x_part, x_part], axis=0))
        total = spread_out[:rows]
        for f in range(1, PER_TILE):
            total = jnp.where(lane_filter == f, spread_out[f * rows : (f + 1) * rows], total)
        y_local[j] = total + skip[pl.ds(j, 1), :] * x_part.astype(F32)
        return carry

    lax.fori_loop(0, tiles, inside, 0, unroll=UNROLL)

    own = iota((MODES, LANES), 1) // GROUP

    def carry_in(source, j, carry):
        states = jnp.concatenate([source[2 * j, 0:8], source[2 * j + 1, 0:8]], axis=0)
        high = states.astype(BF16)
        low = (states - high.astype(F32)).astype(BF16)
        high = [jnp.where(own == f, high, jnp.zeros_like(high)) for f in range(PER_TILE)]
        low = [jnp.where(own == f, low, jnp.zeros_like(low)) for f in range(PER_TILE)]
        y_local[j] += nn(a_out[j], jnp.concatenate(high + high + low, axis=0))
        return carry

    def finish(j, carry):
        cols = pl.ds(pl.multiple_of(j * LANES, LANES), LANES)
        conv = y_local[j].astype(BF16)
        out_ref[:, cols] = (gate[:, cols].astype(F32) * conv.astype(F32)).astype(BF16)
        return carry

    wait_in(lx_in, 4)
    lz_out[...] = ((lx_in[0] + lx_in[1]) + lx_in[2]) + lx_in[3]
    lz_in[z_me] = lz_out[...]
    send_z(lz_out, lz_in, 5)
    wait_in(q_in, 8)
    lax.fori_loop(0, tiles, functools.partial(carry_in, q_in), 0, unroll=UNROLL)

    @pl.when(z_me == 0)
    def first_plane():
        lax.fori_loop(0, tiles, finish, 0, unroll=UNROLL)

    wait_in(z_in, 6)
    entering = zero
    state, second, grad_one, grad_two, packed = zero, zero, zero, zero, zero
    for z in range(planes):
        back_one, back_two, total_one = z_in[z, 8:16], z_in[z, 16:24], z_in[z, 32:40]
        entering = jnp.where(z_me == z, state, entering)
        grad_one += state * back_one
        grad_two += second * back_one + state * back_two
        packed += z_in[z, 24:32]
        second = plane_step * (second + float(rows * plane) * state) + z_in[z, 0:8]
        state = plane_step * state + total_one
    packed += fold(grad_one, grad_two)
    for p in range(plane):
        r_out[p, 0:8] = powers[p] * entering
        r_out[p, 8:16] = packed
    r_in[p_me] = r_out[p_me]
    send_plane(r_out, r_in, 7)

    wait_in(r_in, 7)

    @pl.when(z_me > 0)
    def from_other_planes():
        lax.fori_loop(0, tiles, functools.partial(carry_in, r_in), 0, unroll=UNROLL)
        lax.fori_loop(0, tiles, finish, 0, unroll=UNROLL)

    wait_in(lz_in, 5)
    near = ((lz_in[0] + lz_in[1]) + lz_in[2]) + lz_in[3]
    half_lanes = iota((MODES, LANES), 1) % GROUP < GROUP // 2
    ones, twos = [], []
    for j in range(tiles):
        part = jnp.concatenate([r_in[2 * j, 8:16], r_in[2 * j + 1, 8:16]], axis=0)
        one = jnp.where(lane_mode, near[j : j + 1], 0.0)
        two = jnp.where(lane_mode, near[tiles + j : tiles + j + 1], 0.0)
        ones.append(jnp.where(half_lanes, part, 0.0) + one)
        twos.append(jnp.where(half_lanes, 0.0, part) + two)
    total = jnp.concatenate([jnp.concatenate(ones, axis=1), jnp.concatenate(twos, axis=1)], axis=0)
    grads = nt(thirds(total), own_lanes)
    grads = grads[: 2 * MODES] + grads[2 * MODES : 4 * MODES] + grads[4 * MODES :]
    gres_ref[...] = grads[:MODES] / float(length)
    grate_ref[...] = -(res[...] * jnp.exp(lrate[...]) / float(length)) * grads[MODES:]

    for kind, buffer in enumerate(
        (sq_in, c_in, s_in, ly_in, lx_in, lz_in, z_in, r_in, q_in)
    ):
        wait_out(buffer, kind)


def hand_on(gated, grad_res, grad_rate, gated_hbm, grad_res_hbm, grad_rate_hbm, sem):
    cut = gated.shape[0] // CUTS
    copies = [
        pltpu.make_async_copy(gated.at[pl.ds(cut * k, cut)], gated_hbm.at[pl.ds(cut * k, cut)], sem.at[k])
        for k in range(CUTS)
    ]
    copies.append(pltpu.make_async_copy(grad_res, grad_res_hbm, sem.at[CUTS]))
    copies.append(pltpu.make_async_copy(grad_rate, grad_rate_hbm, sem.at[CUTS + 1]))
    for copy in copies:
        copy.start()
    for copy in copies:
        copy.wait()


def solution(mesh):
    groups = mesh.shape["ch"]
    blocks = mesh.shape["ctx"]
    plane = SIDE * SIDE
    planes = blocks // plane

    def local(features, norm_gain, skip_gain, gate_value, cotangent, residue, log_rate):
        rows, chans = features.shape
        tiles = chans // LANES
        filters = residue.shape[0]
        wide = lambda *shape: pltpu.VMEM(shape, F32)
        half = lambda *shape: pltpu.VMEM(shape, BF16)
        far_spec = pl.BlockSpec(memory_space=pltpu.HBM)
        near_spec = pl.BlockSpec(memory_space=pltpu.VMEM)
        shapes = (
            jax.ShapeDtypeStruct((rows, chans), BF16),
            jax.ShapeDtypeStruct((MODES, filters), F32),
            jax.ShapeDtypeStruct((MODES, filters), F32),
        )
        results = pl.pallas_call(
            functools.partial(body, plane, planes, groups, rows * blocks),
            out_shape=tuple(pltpu.VMEM(part.shape, part.dtype) for part in shapes),
            in_specs=[far_spec] * 7,
            out_specs=(near_spec,) * 3,
            scratch_shapes=[
                half(rows, chans), wide(tiles, LANES), wide(tiles, LANES), half(rows, chans),
                half(rows, chans), wide(MODES, filters), wide(MODES, filters),
                half(tiles, rows, LANES), half(tiles, rows, LANES),
                wide(tiles, 8, LANES), wide(tiles, 8, LANES),
                half(tiles, 2 * LANES, 2 * LANES), half(tiles, LANES, 3 * LANES),
                half(tiles, 2 * rows, LANES), half(tiles, PER_TILE * rows, 2 * LANES),
                wide(plane, 8, LANES), wide(plane, 8, LANES), wide(tiles, rows, LANES),
                wide(tiles, STEP * PER_TILE, LANES),
                wide(1, LANES), wide(groups, 1, LANES),
                wide(plane, 16, LANES), wide(plane, 16, LANES),
                wide(plane, 16, LANES), wide(plane, 16, LANES),
                wide(16, LANES), wide(SIDE, 16, LANES), wide(16, LANES), wide(SIDE, 16, LANES),
                wide(16, LANES), wide(planes, 16, LANES),
                wide(40, LANES), wide(planes, 40, LANES),
                wide(plane, 16, LANES), wide(plane, 16, LANES),
                wide(plane, 8, LANES), wide(plane, 8, LANES),
                pltpu.SemaphoreType.DMA((4 + 3 * CUTS,)),
                pltpu.SemaphoreType.DMA((9,)),
                pltpu.SemaphoreType.DMA((9,)),
                pltpu.SemaphoreType.REGULAR,
                pltpu.SemaphoreType.REGULAR,
            ],
            compiler_params=pltpu.CompilerParams(
                collective_id=0, has_side_effects=True, vmem_limit_bytes=40 * 1024 * 1024
            ),
        )(
            *(
                pltpu.with_memory_space_constraint(part, pltpu.HBM)
                for part in (
                    features,
                    norm_gain.reshape(tiles, LANES),
                    skip_gain.reshape(tiles, LANES),
                    gate_value,
                    cotangent,
                    residue.T,
                    log_rate.T,
                )
            )
        )
        gated, grad_res, grad_rate = pl.pallas_call(
            hand_on,
            out_shape=tuple(pltpu.HBM(part.shape, part.dtype) for part in shapes),
            in_specs=[near_spec] * 3,
            out_specs=(far_spec,) * 3,
            scratch_shapes=[pltpu.SemaphoreType.DMA((CUTS + 2,))],
        )(*(pltpu.with_memory_space_constraint(part, pltpu.VMEM) for part in results))
        return gated, grad_res.T, grad_rate.T

    in_specs = (
        P("ctx", "ch"),
        P("ch"),
        P("ch"),
        P("ctx", "ch"),
        P("ctx", "ch"),
        P("ch", None),
        P("ch", None),
    )
    out_specs = (P("ctx", "ch"), P("ch", None), P("ch", None))
    return jax.shard_map(local, mesh=mesh, in_specs=in_specs, out_specs=out_specs, check_vma=False)
```
